256 devices in a mesh: blk: 256 (over x, y, z, core).
Axes of the slice: x: 4, y: 4, z: 8, core: 2. Of those that a mesh axis runs over, the one named last changes fastest.
Arguments:
- features: bfloat16 [65536, 384], P('blk'), may hold values from -24 to 24
- w_query: bfloat16 [384, 384], replicated, may hold values from -1 to 1
- w_key: bfloat16 [384, 384], replicated, may hold values from -1 to 1
- w_value: bfloat16 [384, 384], replicated, may hold values from -0.3125 to 0.3125
- w_out: bfloat16 [384, 384], replicated, may hold values from -2.5 to 2.5
- cotangent: bfloat16 [65536, 384], P('blk'), may hold values from -6 to 6
- reach: int32 [2, 65536], P(None, 'blk'), may hold values from 1 to 256, as said below
- picks: int32 [2, 256], P(None, 'blk'), may hold values from 0 to 1
- masks: int32 [2], replicated, may hold values from 1 to 255
Outputs:
- mixed: bfloat16 [65536, 384], P('blk')
- feature_grad: bfloat16 [65536, 384], P('blk')
- weight_grads: float32 [4, 384, 384], replicated
The draws below stay inside these ranges and needn't reach their ends.
Inputs may be any that keep to these rules, and one draw needn't show every extreme that they name: `reach`: 256 is reached in every draw. picks[m, d] numbers a block of 128 consecutive nodes of device d. Matching m pairs device d with device d XOR masks[m].
All inputs are finite; a program needn't handle non-finite values.
Results may differ from the reference program's by a relative error of at most 0.011.
Values may be sent and summed in bfloat16 or wider, within the bound.
No kernel may reach another device: no remote copies, remote signals or barrier semaphores. Data moves between devices by JAX's collectives and lax.ppermute only.
A program may use at most 64 MiB of HBM per device.

```python
import jax
import jax.numpy as jnp
from jax import lax

D = 384
HEADS = 8
ROWS_DEV = 256
HALF = 256
BLOCK = 128
MATCH = 2
NODES = 65536
N_BLK = 256


def shared_matrix(key):
    return jax.random.normal(key, (D, D), jnp.float32)


def draw_features(key, part):
    key = jax.random.fold_in(key, 11)
    values = jnp.clip(jax.random.normal(key, (NODES, D), jnp.float32), -6.0, 6.0)
    return values.astype(jnp.bfloat16)


def draw_w_query(key, part):
    shared = shared_matrix(key)
    return (jnp.clip(shared, -5.0, 5.0) * D ** (-0.5)).astype(jnp.bfloat16)


def draw_w_key(key, part):
    key = jax.random.fold_in(key, 22)
    own = jax.random.normal(key, (D, D), jnp.float32)
    values = jnp.clip(own, -5.0, 5.0)
    return (values * D ** (-0.5)).astype(jnp.bfloat16)


def draw_reach(key, part):
    key = jax.random.fold_in(key, 31)
    values = jax.random.randint(key, (2, NODES), 1, HALF + 1, dtype=jnp.int32)
    return values.at[:, 0].set(HALF)


def plant(values, stream_key, least, high):
    index_at = [jax.random.randint(jax.random.fold_in(stream_key, axis), (), 0, length) for axis, length in enumerate(values.shape)]
    main_axis = values.shape.index(max(values.shape))
    next_to = index_at[:main_axis] + [(index_at[main_axis] + 1) % values.shape[main_axis]] + index_at[main_axis + 1:]
    return values.at[tuple(index_at)].set(least).at[tuple(next_to)].set(high)


def steps_of(key, extent, cuts, smallest, high):
    level = 1.0
    for position, blocks in cuts:
        steps = jax.random.uniform(jax.random.fold_in(jax.random.fold_in(key, 6), position), (blocks,), jnp.float32, smallest / len(cuts), high / len(cuts))
        level = level * jnp.repeat(jnp.exp(steps), extent[position] // blocks).reshape((-1,) + (1,) * (len(extent) - 1 - position))
    return level


def normal_values(rng, extent, spread, most, pieces=(), kind=jnp.bfloat16):
    array = jax.random.normal(rng, extent, jnp.float32) * spread
    if len(pieces) > 0:
        array = steps_of(rng, extent, pieces, -0.22, 0.18) * array
    return jnp.clip(array, min=-most, max=most).astype(kind)


def setup_inputs(seed: int = 0) -> dict:
    splits = jax.random.split(jax.random.key(seed), 10)
    return {
        "features": draw_features(jax.random.fold_in(splits[9], 71), 0),
        "w_query": draw_w_query(jax.random.fold_in(splits[9], 71), 0),
        "w_key": draw_w_key(jax.random.fold_in(splits[9], 71), 0),
        "w_value": normal_values(splits[3], (D, D), D ** -0.5, 0.3125),
        "w_out": normal_values(splits[4], (D, D), (D // 64) ** -0.5, 2.5),
        "cotangent": normal_values(splits[5], (NODES, D), 1.0, 6.0, ((0, 256),)),
        "reach": draw_reach(jax.random.fold_in(splits[9], 71), 0),
        "picks": plant(jax.random.randint(splits[7], (MATCH, N_BLK), 0, ROWS_DEV // BLOCK), jax.random.fold_in(splits[7], 1), 0, (ROWS_DEV // BLOCK) - 1).astype(jnp.int32),
        "masks": jax.random.randint(splits[8], (MATCH,), 1, N_BLK).astype(jnp.int32),
    }


def allowed_pairs(left, right, chosen, row_count, half_reach, block_rows, match_count):
    row_ids = jnp.arange(row_count, dtype=jnp.int32)[:, None]
    col_ids = jnp.arange(row_count + 2 * half_reach, dtype=jnp.int32)[None, :]
    offset = col_ids - half_reach - row_ids
    near = (offset >= -left[:, None]) & (offset <= right[:, None])
    far_owner = jnp.arange(match_count * block_rows, dtype=jnp.int32) // block_rows
    block_of_row = jnp.arange(row_count, dtype=jnp.int32) // block_rows
    far = block_of_row[:, None] == chosen[far_owner][None, :]
    return jnp.concatenate([near, far], axis=1)


def attend(queries, keys_all, dattn, allowed):
    row_count, feat_width = queries.shape
    key_count = keys_all.shape[0]
    head_dim = feat_width // HEADS
    factor = head_dim ** -0.5
    q_heads = queries.reshape(row_count, HEADS, head_dim).transpose(1, 0, 2)
    k_heads = keys_all[:, :feat_width].reshape(key_count, HEADS, head_dim).transpose(1, 0, 2)
    v_heads = keys_all[:, feat_width:].reshape(key_count, HEADS, head_dim).transpose(1, 0, 2)
    d_heads = dattn.reshape(row_count, HEADS, head_dim).transpose(1, 0, 2)

    def one_head(operands):
        q_head, k_head, v_head, d_head = operands
        scores = jnp.dot(q_head, k_head.T, preferred_element_type=jnp.float32) * factor
        scores = jnp.where(allowed, scores, -1e30)
        largest = jnp.max(scores, axis=1, keepdims=True)
        raised = jnp.where(allowed, jnp.exp(scores - largest), 0.0)
        prob_f32 = raised / jnp.sum(raised, axis=1, keepdims=True)
        prob_b16 = prob_f32.astype(jnp.bfloat16)
        attn_head = jnp.dot(prob_b16, v_head, preferred_element_type=jnp.float32)
        dprob = jnp.dot(d_head, v_head.T, preferred_element_type=jnp.float32)
        mean_term = jnp.sum(prob_f32 * dprob, axis=1, keepdims=True)
        dscore = (prob_f32 * (dprob - mean_term) * factor).astype(jnp.bfloat16)
        dq_head = jnp.dot(dscore, k_head, preferred_element_type=jnp.float32)
        dk_head = jnp.dot(dscore.T, q_head, preferred_element_type=jnp.float32)
        dv_head = jnp.dot(prob_b16.T, d_head, preferred_element_type=jnp.float32)
        return attn_head, dq_head, dk_head, dv_head

    attn_all, dq_all, dk_all, dv_all = lax.map(one_head, (q_heads, k_heads, v_heads, d_heads))
    attention = attn_all.transpose(1, 0, 2).reshape(row_count, feat_width).astype(jnp.bfloat16)
    query_grad = dq_all.transpose(1, 0, 2).reshape(row_count, feat_width).astype(jnp.bfloat16)
    key_grad = dk_all.transpose(1, 0, 2).reshape(key_count, feat_width)
    value_grad = dv_all.transpose(1, 0, 2).reshape(key_count, feat_width)
    return attention, query_grad, jnp.concatenate([key_grad, value_grad], axis=1)


def reference(features, w_query, w_key, w_value, w_out, cotangent, reach, picks, masks):
    node_count, feat_width = features.shape
    row_count = node_count // N_BLK
    half_reach = HALF
    ext_rows = row_count + 2 * half_reach
    w_pair = jnp.concatenate([w_key, w_value], axis=1)
    w_pair_wide = w_pair.astype(jnp.float32)
    queries = jnp.dot(features, w_query, preferred_element_type=jnp.float32).astype(jnp.bfloat16)
    key_values = jnp.dot(features, w_pair, preferred_element_type=jnp.float32).astype(jnp.bfloat16)
    dattn = jnp.dot(cotangent, w_out.T, preferred_element_type=jnp.float32).astype(jnp.bfloat16)
    padded = jnp.concatenate([key_values[node_count - half_reach:], key_values, key_values[:half_reach]], axis=0)
    far_blocks = key_values.reshape(N_BLK, row_count // BLOCK, BLOCK, 2 * feat_width)
    match_ids = jnp.arange(MATCH, dtype=jnp.int32)

    def per_device(carry, device):
        start = (device * row_count).astype(jnp.int32)
        q_rows = lax.dynamic_slice_in_dim(queries, start, row_count, 0)
        near_rows = lax.dynamic_slice_in_dim(padded, start, ext_rows, 0)
        chosen = picks[:, device]
        partners = jnp.bitwise_xor(device, masks).astype(jnp.int32)
        their = picks[match_ids, partners]
        remote = far_blocks[partners, their].reshape(MATCH * BLOCK, 2 * feat_width)
        keys_all = jnp.concatenate([near_rows, remote], axis=0)
        left = lax.dynamic_slice_in_dim(reach[0], start, row_count, 0)
        right = lax.dynamic_slice_in_dim(reach[1], start, row_count, 0)
        allowed = allowed_pairs(left, right, chosen, row_count, half_reach, BLOCK, MATCH)
        d_rows = lax.dynamic_slice_in_dim(dattn, start, row_count, 0)
        attention, query_grad, pair_grad = attend(q_rows, keys_all, d_rows, allowed)
        current = lax.dynamic_slice_in_dim(carry, start, ext_rows, 0)
        carry = lax.dynamic_update_slice_in_dim(carry, current + pair_grad[:ext_rows], start, 0)
        for matching in range(MATCH):
            spot = (half_reach + partners[matching] * row_count + their[matching] * BLOCK).astype(jnp.int32)
            piece = lax.dynamic_slice_in_dim(carry, spot, BLOCK, 0)
            lower = ext_rows + matching * BLOCK
            carry = lax.dynamic_update_slice_in_dim(carry, piece + pair_grad[lower:lower + BLOCK], spot, 0)
        return carry, (attention, query_grad)

    initial = jnp.zeros((node_count + 2 * half_reach, 2 * feat_width), jnp.float32)
    carry, (attention, query_grad) = lax.scan(per_device, initial, jnp.arange(N_BLK, dtype=jnp.int32))
    attention = attention.reshape(node_count, feat_width)
    query_grad = query_grad.reshape(node_count, feat_width)
    pair_sum = carry[half_reach:half_reach + node_count]
    pair_sum = pair_sum.at[:half_reach].add(carry[half_reach + node_count:])
    pair_sum = pair_sum.at[node_count - half_reach:].add(carry[:half_reach])
    mixed = jnp.dot(attention, w_out, preferred_element_type=jnp.float32).astype(jnp.bfloat16)
    feature_grad = (jnp.dot(query_grad, w_query.T, preferred_element_type=jnp.float32)
                    + jnp.dot(pair_sum, w_pair_wide.T, precision=lax.Precision.HIGHEST)).astype(jnp.bfloat16)
    grad_query = jnp.dot(features.T, query_grad, preferred_element_type=jnp.float32)
    grad_pair = jnp.dot(features.astype(jnp.float32).T, pair_sum, precision=lax.Precision.HIGHEST)
    grad_out = jnp.dot(attention.T, cotangent, preferred_element_type=jnp.float32)
    stacked = jnp.stack([grad_query, grad_pair[:, :feat_width], grad_pair[:, feat_width:], grad_out])
    grad_scale = float(node_count) ** -0.5
    return mixed, feature_grad, stacked * grad_scale
```

```python
import jax
import jax.numpy as jnp
from jax import lax
from jax.experimental import pallas as pl
from jax.experimental.pallas import tpu as pltpu
from jax.sharding import PartitionSpec as P

HEADS = 8
HALF = 256
BLOCK = 128
MATCH = 2
ROWS = 256
D = 384
HD = D // HEADS
NEAR = ROWS + 2 * HALF
KEYS = NEAR + MATCH * BLOCK
PIECES = KEYS // ROWS
CHUNK = 128
FACTOR = HD ** -0.5
LOG2E = 1.4426950408889634
AXIS = "blk"
PLANE = 16
LINE = 16
PART = 4 * D // PLANE
DIGIT = 4
F32 = jnp.float32
BF16 = jnp.bfloat16


def nn(a, b):
    return lax.dot_general(a, b, (((1,), (0,)), ((), ())), preferred_element_type=F32)


def nt(a, b):
    return lax.dot_general(a, b, (((1,), (1,)), ((), ())), preferred_element_type=F32)


def tn(a, b):
    return lax.dot_general(a, b, (((0,), (0,)), ((), ())), preferred_element_type=F32)


def attend_kernel(
    picks_ref, reach_ref, prev_ref, own_ref, next_ref, far0_ref, far1_ref, cot_ref,
    wq_ref, wk_ref, wv_ref, wo_ref,
    mixed_ref, f_own_ref, f_prev_ref, f_next_ref, f_far0_ref, f_far1_ref, wg_ref,
    x_all, w_t, qt, dt, kt, vt, bias, s_ref, dp_ref, pb, dsb, ot, dqt, dkt, dvt, f_all, g_sum,
):
    x_all[0] = prev_ref[...]
    x_all[1] = own_ref[...]
    x_all[2] = next_ref[...]
    x_all[3, 0:BLOCK, :] = far0_ref[...]
    x_all[3, BLOCK:, :] = far1_ref[...]
    w_t[0] = wq_ref[...].T
    w_t[1] = wk_ref[...].T
    w_t[2] = wv_ref[...].T
    qt[...] = nt(w_t[0], own_ref[...]).astype(BF16)
    dt[...] = nt(wo_ref[...], cot_ref[...]).astype(BF16)

    def project(i, _):
        span = pl.ds(pl.multiple_of(i * ROWS, ROWS), ROWS)
        kt[:, span] = nt(w_t[1], x_all[i]).astype(BF16)
        vt[:, span] = nt(w_t[2], x_all[i]).astype(BF16)
        return 0

    lax.fori_loop(0, PIECES, project, 0)

    rows = lax.broadcasted_iota(jnp.int32, (CHUNK, ROWS), 1)
    cols = lax.broadcasted_iota(jnp.int32, (CHUNK, ROWS), 0)
    offset = cols - HALF - rows
    back = -reach_ref[0:1, :]
    ahead = reach_ref[1:2, :]

    def near_bias(c, _):
        start = pl.multiple_of(c * CHUNK, CHUNK)
        allowed = (offset >= back - start) & (offset <= ahead - start)
        bias[pl.ds(start, CHUNK), :] = jnp.where(allowed, 0.0, -1e30)
        return 0

    lax.fori_loop(0, NEAR // CHUNK, near_bias, 0)
    for m in range(MATCH):
        allowed = rows // BLOCK == picks_ref[0, m]
        at = NEAR + m * BLOCK
        bias[at:at + BLOCK, :] = jnp.where(allowed, 0.0, -1e30)

    chunks = [slice(c * CHUNK, (c + 1) * CHUNK) for c in range(KEYS // CHUNK)]

    def one_head(h, _):
        at = pl.ds(pl.multiple_of(h * HD, HD), HD)
        q_h, d_h, k_h, v_h = qt[at, :], dt[at, :], kt[at, :], vt[at, :]
        top = jnp.full((8, ROWS), -3e38, F32)
        for c in chunks:
            s = tn(k_h[:, c], q_h) + bias[c, :]
            s_ref[c, :] = s
            top = jnp.maximum(top, jnp.max(s.reshape(CHUNK // 8, 8, ROWS), axis=0))
        top = jnp.max(top, axis=0, keepdims=True)
        total = jnp.zeros((8, ROWS), F32)
        mean = jnp.zeros((8, ROWS), F32)
        for c in chunks:
            e = jnp.exp2((s_ref[c, :] - top) * (FACTOR * LOG2E))
            s_ref[c, :] = e
            dp = tn(v_h[:, c], d_h)
            dp_ref[c, :] = dp
            total += jnp.sum(e.reshape(CHUNK // 8, 8, ROWS), axis=0)
            mean += jnp.sum((e * dp).reshape(CHUNK // 8, 8, ROWS), axis=0)
        inverse = 1.0 / jnp.sum(total, axis=0, keepdims=True)
        mean = jnp.sum(mean, axis=0, keepdims=True) * inverse
        for c in chunks:
            p = s_ref[c, :] * inverse
            pb[c, :] = p.astype(BF16)
            dsb[c, :] = (p * (dp_ref[c, :] - mean) * FACTOR).astype(BF16)
        ot[at, :] = nn(v_h, pb[...]).astype(BF16)
        dvt[at, :] = nt(d_h, pb[...]).astype(BF16)
        dqt[at, :] = nn(k_h, dsb[...]).astype(BF16)
        dkt[at, :] = nt(q_h, dsb[...]).astype(BF16)
        return 0

    lax.fori_loop(0, HEADS, one_head, 0)

    g_sum[...] = jnp.zeros_like(g_sum)

    def collect(i, _):
        span = pl.ds(pl.multiple_of(i * ROWS, ROWS), ROWS)
        f_all[i] = tn(dkt[:, span], w_t[1]) + tn(dvt[:, span], w_t[2])
        g_sum[0] += nn(dkt[:, span], x_all[i])
        g_sum[1] += nn(dvt[:, span], x_all[i])
        return 0

    lax.fori_loop(0, PIECES, collect, 0)

    mixed_ref[...] = tn(ot[...], wo_ref[...]).astype(BF16)
    f_own_ref[...] = f_all[1] + tn(dqt[...], w_t[0])
    f_prev_ref[...] = f_all[0].astype(BF16)
    f_next_ref[...] = f_all[2].astype(BF16)
    f_far0_ref[...] = f_all[3, 0:BLOCK, :].astype(BF16)
    f_far1_ref[...] = f_all[3, BLOCK:, :].astype(BF16)
    scale = float(ROWS * 256) ** -0.5
    grads = (
        (nn(dqt[...], own_ref[...]) * scale).T,
        (g_sum[0] * scale).T,
        (g_sum[1] * scale).T,
        nn(ot[...], cot_ref[...]) * scale,
    )
    for i, grad in enumerate(grads):
        wg_ref[i * D:(i + 1) * D, :] = grad.astype(BF16)


def attend(picks, reach, prev, own, following, far0, far1, cot, wq, wk, wv, wo):
    vmem = pl.BlockSpec(memory_space=pltpu.VMEM)
    smem = pl.BlockSpec(memory_space=pltpu.SMEM)
    shape = jax.ShapeDtypeStruct
    return pl.pallas_call(
        attend_kernel,
        out_shape=(
            shape((ROWS, D), BF16),
            shape((ROWS, D), F32),
            shape((HALF, D), BF16),
            shape((HALF, D), BF16),
            shape((BLOCK, D), BF16),
            shape((BLOCK, D), BF16),
            shape((4 * D, D), BF16),
        ),
        in_specs=[smem] + [vmem] * 11,
        out_specs=(vmem,) * 7,
        scratch_shapes=[
            pltpu.VMEM((PIECES, ROWS, D), BF16),
            pltpu.VMEM((3, D, D), BF16),
            pltpu.VMEM((D, ROWS), BF16),
            pltpu.VMEM((D, ROWS), BF16),
            pltpu.VMEM((D, KEYS), BF16),
            pltpu.VMEM((D, KEYS), BF16),
            pltpu.VMEM((KEYS, ROWS), F32),
            pltpu.VMEM((KEYS, ROWS), F32),
            pltpu.VMEM((KEYS, ROWS), F32),
            pltpu.VMEM((KEYS, ROWS), BF16),
            pltpu.VMEM((KEYS, ROWS), BF16),
            pltpu.VMEM((D, ROWS), BF16),
            pltpu.VMEM((D, ROWS), BF16),
            pltpu.VMEM((D, KEYS), BF16),
            pltpu.VMEM((D, KEYS), BF16),
            pltpu.VMEM((PIECES, ROWS, D), F32),
            pltpu.VMEM((2, D, D), F32),
        ],
        compiler_params=pltpu.CompilerParams(vmem_limit_bytes=40 * 1024 * 1024),
        cost_estimate=pl.CostEstimate(
            flops=8_000_000_000, bytes_accessed=8_000_000, transcendentals=HEADS * KEYS * ROWS
        ),
    )(picks, reach, prev, own, following, far0, far1, cot, wq, wk, wv, wo)


def crossed(block, mask, digit):
    count = lax.axis_size(AXIS)
    bits = count.bit_length() - 1

    def move(offset):
        pairs = [(i, i ^ offset) for i in range(count)]
        return lambda piece: lax.ppermute(piece, AXIS, pairs) if offset else piece

    for low in range(0, bits, digit):
        value = (mask >> low) & ((1 << digit) - 1)
        block = lax.switch(value, [move(i << low) for i in range(1 << digit)], block)
    return block


def across(block, offset):
    return lax.ppermute(block, AXIS, [(i, i ^ offset) for i in range(lax.axis_size(AXIS))])


def tree(values):
    while len(values) > 1:
        values = [a + b for a, b in zip(values[::2], values[1::2])]
    return values[0]


def total_of(partial):
    planes = [[i * LINE + j for i in range(PLANE)] for j in range(LINE)]
    parts = lax.all_to_all(partial.reshape(PLANE, PART, D), AXIS, 0, 0, axis_index_groups=planes)
    mine = tree([parts[i].astype(F32) for i in range(PLANE)]).astype(BF16)
    for step in (1, 4):
        terms = [mine] + [across(mine, o * step) for o in range(1, 4)]
        mine = tree([term.astype(F32) for term in terms]).astype(BF16)
    copies = jnp.broadcast_to(mine[None], (PLANE, PART, D))
    return lax.all_to_all(copies, AXIS, 0, 0, axis_index_groups=planes)


def finish_kernel(picks_ref, own_ref, from_next_ref, from_prev_ref, far0_ref, far1_ref, total_ref, f_ref, wg_ref):
    far = [ref[...].astype(F32) for ref in (far0_ref, far1_ref)]
    for b in range(ROWS // BLOCK):
        span = slice(b * BLOCK, (b + 1) * BLOCK)
        value = own_ref[span, :] + from_next_ref[span, :].astype(F32) + from_prev_ref[span, :].astype(F32)
        for m in range(MATCH):
            value += jnp.where(picks_ref[0, m] == b, far[m], 0.0)
        f_ref[span, :] = value.astype(BF16)

    def widen(i, _):
        wg_ref[i] = total_ref[i].astype(F32)
        return 0

    lax.fori_loop(0, PLANE, widen, 0)


def finish(picks, own, from_next, from_prev, far0, far1, total):
    vmem = pl.BlockSpec(memory_space=pltpu.VMEM)
    smem = pl.BlockSpec(memory_space=pltpu.SMEM)
    shape = jax.ShapeDtypeStruct
    return pl.pallas_call(
        finish_kernel,
        out_shape=(shape((ROWS, D), BF16), shape((PLANE, PART, D), F32)),
        in_specs=[smem] + [vmem] * 6,
        out_specs=(vmem, vmem),
        compiler_params=pltpu.CompilerParams(vmem_limit_bytes=16 * 1024 * 1024),
    )(picks, own, from_next, from_prev, far0, far1, total)


def shards(features, w_query, w_key, w_value, w_out, cotangent, reach, picks, masks):
    count = lax.axis_size(AXIS)
    bits = count.bit_length() - 1
    up = [(i, (i + 1) % count) for i in range(count)]
    down = [(j, i) for i, j in up]
    picked = picks.reshape(1, MATCH)
    prev = lax.ppermute(features, AXIS, up)
    following = lax.ppermute(features, AXIS, down)
    halves = features.reshape(ROWS // BLOCK, BLOCK, D)
    outgoing = jnp.where(picks[:, :, None] == 0, halves[0][None], halves[1][None])
    both = jnp.sum(masks * jnp.array([1, count]))
    routes = [(both >> (m * bits)) & (count - 1) for m in range(MATCH)]
    far = [crossed(outgoing[m], routes[m], DIGIT) for m in range(MATCH)]
    mixed, f_own, f_prev, f_next, f_far0, f_far1, partial = attend(
        picked, reach, prev, features, following, far[0], far[1], cotangent,
        w_query, w_key, w_value, w_out,
    )
    from_next = lax.ppermute(f_prev, AXIS, down)
    from_prev = lax.ppermute(f_next, AXIS, up)
    far = [crossed(part, route, DIGIT) for part, route in zip((f_far0, f_far1), routes)]
    total = total_of(partial)
    feature_grad, weight_grads = finish(picked, f_own, from_next, from_prev, far[0], far[1], total)
    return mixed, feature_grad, weight_grads.reshape(4, D, D)


def solution(mesh):
    return jax.shard_map(
        shards,
        mesh=mesh,
        in_specs=(
            P("blk", None),
            P(),
            P(),
            P(),
            P(),
            P("blk", None),
            P(None, "blk"),
            P(None, "blk"),
            P(),
        ),
        out_specs=(P("blk", None), P("blk", None), P()),
        check_vma=False,
    )
```

```python
import jax
import jax.numpy as jnp
from jax import lax
from jax.experimental import pallas as pl
from jax.experimental.pallas import tpu as pltpu
from jax.sharding import PartitionSpec as P

HEADS = 8
HALF = 256
BLOCK = 128
MATCH = 2
ROWS = 256
D = 384
HD = D // HEADS
NEAR = ROWS + 2 * HALF
KEYS = NEAR + MATCH * BLOCK
PIECES = KEYS // ROWS
CHUNK = 128
FACTOR = HD ** -0.5
LOG2E = 1.4426950408889634
AXIS = "blk"
PLANE = 16
LINE = 16
GROUP = 64
PART = 4 * D // GROUP
DIGIT = 4
F32 = jnp.float32
BF16 = jnp.bfloat16


def nn(a, b):
    return lax.dot_general(a, b, (((1,), (0,)), ((), ())), preferred_element_type=F32)


def nt(a, b):
    return lax.dot_general(a, b, (((1,), (1,)), ((), ())), preferred_element_type=F32)


def tn(a, b):
    return lax.dot_general(a, b, (((0,), (0,)), ((), ())), preferred_element_type=F32)


def attend_kernel(
    picks_ref, reach_ref, prev_ref, own_ref, next_ref, far0_ref, far1_ref, cot_ref,
    wq_ref, wk_ref, wv_ref, wo_ref,
    mixed_ref, f_own_ref, f_prev_ref, f_next_ref, f_far0_ref, f_far1_ref, wg_ref,
    x_all, w_t, qt, dt, kt, vt, bias, s_ref, dp_ref, pb, dsb, ot, dqt, dkt, dvt, f_all, g_sum,
):
    x_all[0] = prev_ref[...]
    x_all[1] = own_ref[...]
    x_all[2] = next_ref[...]
    x_all[3, 0:BLOCK, :] = far0_ref[...]
    x_all[3, BLOCK:, :] = far1_ref[...]
    w_t[0] = wq_ref[...].T
    w_t[1] = wk_ref[...].T
    w_t[2] = wv_ref[...].T
    qt[...] = nt(w_t[0], own_ref[...]).astype(BF16)
    dt[...] = nt(wo_ref[...], cot_ref[...]).astype(BF16)

    def project(i, _):
        span = pl.ds(pl.multiple_of(i * ROWS, ROWS), ROWS)
        kt[:, span] = nt(w_t[1], x_all[i]).astype(BF16)
        vt[:, span] = nt(w_t[2], x_all[i]).astype(BF16)
        return 0

    lax.fori_loop(0, PIECES, project, 0)

    rows = lax.broadcasted_iota(jnp.int32, (CHUNK, ROWS), 1)
    cols = lax.broadcasted_iota(jnp.int32, (CHUNK, ROWS), 0)
    offset = cols - HALF - rows
    back = -reach_ref[0:1, :]
    ahead = reach_ref[1:2, :]

    def near_bias(c, _):
        start = pl.multiple_of(c * CHUNK, CHUNK)
        allowed = (offset >= back - start) & (offset <= ahead - start)
        bias[pl.ds(start, CHUNK), :] = jnp.where(allowed, 0.0, -1e30)
        return 0

    lax.fori_loop(0, NEAR // CHUNK, near_bias, 0)
    for m in range(MATCH):
        allowed = rows // BLOCK == picks_ref[0, m]
        at = NEAR + m * BLOCK
        bias[at:at + BLOCK, :] = jnp.where(allowed, 0.0, -1e30)

    chunks = [slice(c * CHUNK, (c + 1) * CHUNK) for c in range(KEYS // CHUNK)]

    def one_head(h, _):
        at = pl.ds(pl.multiple_of(h * HD, HD), HD)
        q_h, d_h, k_h, v_h = qt[at, :], dt[at, :], kt[at, :], vt[at, :]
        top = jnp.full((8, ROWS), -3e38, F32)
        for c in chunks:
            s = tn(k_h[:, c], q_h) + bias[c, :]
            s_ref[c, :] = s
            top = jnp.maximum(top, jnp.max(s.reshape(CHUNK // 8, 8, ROWS), axis=0))
        top = jnp.max(top, axis=0, keepdims=True)
        total = jnp.zeros((8, ROWS), F32)
        mean = jnp.zeros((8, ROWS), F32)
        for c in chunks:
            e = jnp.exp2((s_ref[c, :] - top) * (FACTOR * LOG2E))
            s_ref[c, :] = e
            dp = tn(v_h[:, c], d_h)
            dp_ref[c, :] = dp
            total += jnp.sum(e.reshape(CHUNK // 8, 8, ROWS), axis=0)
            mean += jnp.sum((e * dp).reshape(CHUNK // 8, 8, ROWS), axis=0)
        inverse = 1.0 / jnp.sum(total, axis=0, keepdims=True)
        mean = jnp.sum(mean, axis=0, keepdims=True) * inverse
        for c in chunks:
            p = s_ref[c, :] * inverse
            pb[c, :] = p.astype(BF16)
            dsb[c, :] = (p * (dp_ref[c, :] - mean) * FACTOR).astype(BF16)
        ot[at, :] = nn(v_h, pb[...]).astype(BF16)
        dvt[at, :] = nt(d_h, pb[...]).astype(BF16)
        dqt[at, :] = nn(k_h, dsb[...]).astype(BF16)
        dkt[at, :] = nt(q_h, dsb[...]).astype(BF16)
        return 0

    lax.fori_loop(0, HEADS, one_head, 0)

    g_sum[...] = jnp.zeros_like(g_sum)

    def collect(i, _):
        span = pl.ds(pl.multiple_of(i * ROWS, ROWS), ROWS)
        f_all[i] = tn(dkt[:, span], w_t[1]) + tn(dvt[:, span], w_t[2])
        g_sum[0] += nn(dkt[:, span], x_all[i])
        g_sum[1] += nn(dvt[:, span], x_all[i])
        return 0

    lax.fori_loop(0, PIECES, collect, 0)

    mixed_ref[...] = tn(ot[...], wo_ref[...]).astype(BF16)
    f_own_ref[...] = f_all[1] + tn(dqt[...], w_t[0])
    f_prev_ref[...] = f_all[0].astype(BF16)
    f_next_ref[...] = f_all[2].astype(BF16)
    f_far0_ref[...] = f_all[3, 0:BLOCK, :].astype(BF16)
    f_far1_ref[...] = f_all[3, BLOCK:, :].astype(BF16)
    scale = float(ROWS * 256) ** -0.5
    grads = (
        (nn(dqt[...], own_ref[...]) * scale).T,
        (g_sum[0] * scale).T,
        (g_sum[1] * scale).T,
        nn(ot[...], cot_ref[...]) * scale,
    )
    for i, grad in enumerate(grads):
        wg_ref[i * D:(i + 1) * D, :] = grad.astype(BF16)


def attend(picks, reach, prev, own, following, far0, far1, cot, wq, wk, wv, wo):
    vmem = pl.BlockSpec(memory_space=pltpu.VMEM)
    smem = pl.BlockSpec(memory_space=pltpu.SMEM)
    shape = jax.ShapeDtypeStruct
    return pl.pallas_call(
        attend_kernel,
        out_shape=(
            shape((ROWS, D), BF16),
            shape((ROWS, D), F32),
            shape((HALF, D), BF16),
            shape((HALF, D), BF16),
            shape((BLOCK, D), BF16),
            shape((BLOCK, D), BF16),
            shape((4 * D, D), BF16),
        ),
        in_specs=[smem] + [vmem] * 11,
        out_specs=(vmem,) * 7,
        scratch_shapes=[
            pltpu.VMEM((PIECES, ROWS, D), BF16),
            pltpu.VMEM((3, D, D), BF16),
            pltpu.VMEM((D, ROWS), BF16),
            pltpu.VMEM((D, ROWS), BF16),
            pltpu.VMEM((D, KEYS), BF16),
            pltpu.VMEM((D, KEYS), BF16),
            pltpu.VMEM((KEYS, ROWS), F32),
            pltpu.VMEM((KEYS, ROWS), F32),
            pltpu.VMEM((KEYS, ROWS), F32),
            pltpu.VMEM((KEYS, ROWS), BF16),
            pltpu.VMEM((KEYS, ROWS), BF16),
            pltpu.VMEM((D, ROWS), BF16),
            pltpu.VMEM((D, ROWS), BF16),
            pltpu.VMEM((D, KEYS), BF16),
            pltpu.VMEM((D, KEYS), BF16),
            pltpu.VMEM((PIECES, ROWS, D), F32),
            pltpu.VMEM((2, D, D), F32),
        ],
        compiler_params=pltpu.CompilerParams(vmem_limit_bytes=40 * 1024 * 1024),
        cost_estimate=pl.CostEstimate(
            flops=8_000_000_000, bytes_accessed=8_000_000, transcendentals=HEADS * KEYS * ROWS
        ),
    )(picks, reach, prev, own, following, far0, far1, cot, wq, wk, wv, wo)


def crossed(block, mask, digit):
    count = lax.axis_size(AXIS)
    bits = count.bit_length() - 1

    def move(offset):
        pairs = [(i, i ^ offset) for i in range(count)]
        return lambda piece: lax.ppermute(piece, AXIS, pairs) if offset else piece

    for low in range(0, bits, digit):
        value = (mask >> low) & ((1 << digit) - 1)
        block = lax.switch(value, [move(i << low) for i in range(1 << digit)], block)
    return block


def across(block, offset):
    return lax.ppermute(block, AXIS, [(i, i ^ offset) for i in range(lax.axis_size(AXIS))])


def tree(values):
    while len(values) > 1:
        values = [a + b for a, b in zip(values[::2], values[1::2])]
    return values[0]


def total_of(partial):
    count = lax.axis_size(AXIS)
    low = GROUP // PLANE
    groups = [[i * LINE + j * low + k for i in range(PLANE) for k in range(low)] for j in range(LINE // low)]
    parts = lax.all_to_all(partial.reshape(GROUP, PART, D), AXIS, 0, 0, axis_index_groups=groups)
    mine = tree([parts[i].astype(F32) for i in range(GROUP)]).astype(BF16)
    terms = [mine] + [across(mine, o * low) for o in range(1, count // GROUP)]
    mine = tree([term.astype(F32) for term in terms]).astype(BF16)

    def gather(mine):
        copies = jnp.broadcast_to(mine[None], (GROUP, PART, D))
        return lax.all_to_all(copies, AXIS, 0, 0, axis_index_groups=groups)

    return mine, gather


def finish_kernel(picks_ref, own_ref, from_next_ref, from_prev_ref, far0_ref, far1_ref, total_ref, f_ref, wg_ref):
    far = [ref[...].astype(F32) for ref in (far0_ref, far1_ref)]
    for b in range(ROWS // BLOCK):
        span = slice(b * BLOCK, (b + 1) * BLOCK)
        value = own_ref[span, :] + from_next_ref[span, :].astype(F32) + from_prev_ref[span, :].astype(F32)
        for m in range(MATCH):
            value += jnp.where(picks_ref[0, m] == b, far[m], 0.0)
        f_ref[span, :] = value.astype(BF16)

    def widen(i, _):
        wg_ref[i] = total_ref[i].astype(F32)
        return 0

    lax.fori_loop(0, GROUP, widen, 0)


def finish(picks, own, from_next, from_prev, far0, far1, total):
    vmem = pl.BlockSpec(memory_space=pltpu.VMEM)
    smem = pl.BlockSpec(memory_space=pltpu.SMEM)
    shape = jax.ShapeDtypeStruct
    return pl.pallas_call(
        finish_kernel,
        out_shape=(shape((ROWS, D), BF16), shape((GROUP, PART, D), F32)),
        in_specs=[smem] + [vmem] * 6,
        out_specs=(vmem, vmem),
        compiler_params=pltpu.CompilerParams(vmem_limit_bytes=16 * 1024 * 1024),
    )(picks, own, from_next, from_prev, far0, far1, total)


def shards(features, w_query, w_key, w_value, w_out, cotangent, reach, picks, masks):
    count = lax.axis_size(AXIS)
    bits = count.bit_length() - 1
    up = [(i, (i + 1) % count) for i in range(count)]
    down = [(j, i) for i, j in up]
    picked = picks.reshape(1, MATCH)
    prev = lax.ppermute(features, AXIS, up)
    following = lax.ppermute(features, AXIS, down)
    halves = features.reshape(ROWS // BLOCK, BLOCK, D)
    outgoing = jnp.where(picks[:, :, None] == 0, halves[0][None], halves[1][None])
    both = jnp.sum(masks * jnp.array([1, count]))
    routes = [(both >> (m * bits)) & (count - 1) for m in range(MATCH)]
    far = [crossed(outgoing[m], routes[m], DIGIT) for m in range(MATCH)]
    mixed, f_own, f_prev, f_next, f_far0, f_far1, partial = attend(
        picked, reach, prev, features, following, far[0], far[1], cotangent,
        w_query, w_key, w_value, w_out,
    )
    from_next = lax.ppermute(f_prev, AXIS, down)
    from_prev = lax.ppermute(f_next, AXIS, up)
    mine, gather = total_of(partial)
    mine, f_far0, f_far1 = lax.optimization_barrier((mine, f_far0, f_far1))
    total = gather(mine)
    far = [crossed(part, route, DIGIT) for part, route in zip((f_far0, f_far1), routes)]
    feature_grad, weight_grads = finish(picked, f_own, from_next, from_prev, far[0], far[1], total)
    return mixed, feature_grad, weight_grads.reshape(4, D, D)


def solution(mesh):
    return jax.shard_map(
        shards,
        mesh=mesh,
        in_specs=(
            P("blk", None),
            P(),
            P(),
            P(),
            P(),
            P("blk", None),
            P(None, "blk"),
            P(None, "blk"),
            P(),
        ),
        out_specs=(P("blk", None), P("blk", None), P()),
        check_vma=False,
    )
```

```python
import jax
import jax.numpy as jnp
from jax import lax
from jax.experimental import pallas as pl
from jax.experimental.pallas import tpu as pltpu
from jax.sharding import PartitionSpec as P

HEADS = 8
HALF = 256
BLOCK = 128
MATCH = 2
ROWS = 256
D = 384
HD = D // HEADS
NEAR = ROWS + 2 * HALF
KEYS = NEAR + MATCH * BLOCK
CHUNK = 128
FACTOR = HD ** -0.5
LOG2E = 1.4426950408889634
AXIS = "blk"
PLANE = 16
LINE = 16
GROUP = 64
PART = 4 * D // GROUP
DIGIT = 4
F32 = jnp.float32
BF16 = jnp.bfloat16


def nn(a, b):
    return lax.dot_general(a, b, (((1,), (0,)), ((), ())), preferred_element_type=F32)


def nt(a, b):
    return lax.dot_general(a, b, (((1,), (1,)), ((), ())), preferred_element_type=F32)


def tn(a, b):
    return lax.dot_general(a, b, (((0,), (0,)), ((), ())), preferred_element_type=F32)


def attend_kernel(
    picks_ref, reach_ref, prev_ref, own_ref, next_ref, far0_ref, far1_ref, cot_ref,
    wq_ref, wk_ref, wv_ref, wo_ref,
    mixed_ref, f_own_ref, f_prev_ref, f_next_ref, f_far0_ref, f_far1_ref, wg_ref,
    xt, qt, dt, kt, vt, bias, s_ref, dp_ref, pb, dsb, ot, dqt, dkt, dvt, ft,
):
    own = slice(HALF, HALF + ROWS)
    starts = (0, HALF, HALF + ROWS, NEAR, NEAR + BLOCK)
    for start, piece in zip(starts, (prev_ref, own_ref, next_ref, far0_ref, far1_ref)):
        xt[:, start:start + piece.shape[0]] = piece[...].T
    qt[...] = nn(wq_ref[...].T, xt[:, own]).astype(BF16)
    dt[...] = nt(wo_ref[...], cot_ref[...]).astype(BF16)
    kt[...] = nn(wk_ref[...].T, xt[...]).astype(BF16)
    vt[...] = nn(wv_ref[...].T, xt[...]).astype(BF16)

    rows = lax.broadcasted_iota(jnp.int32, (CHUNK, ROWS), 1)
    cols = lax.broadcasted_iota(jnp.int32, (CHUNK, ROWS), 0)
    offset = cols - HALF - rows
    back = -reach_ref[0:1, :]
    ahead = reach_ref[1:2, :]

    def near_bias(c, _):
        start = pl.multiple_of(c * CHUNK, CHUNK)
        allowed = (offset >= back - start) & (offset <= ahead - start)
        bias[pl.ds(start, CHUNK), :] = jnp.where(allowed, 0.0, -1e30)
        return 0

    lax.fori_loop(0, NEAR // CHUNK, near_bias, 0)

    halves = [slice(0, BLOCK), slice(BLOCK, ROWS)]
    near = [(c, b) for c in range(NEAR // CHUNK) for b in range(2) if b * BLOCK <= c * CHUNK <= b * BLOCK + 2 * HALF]
    picked = [picks_ref[0, m] for m in range(MATCH)]
    far_rows = [pl.ds(pl.multiple_of(picked[m] * BLOCK, BLOCK), BLOCK) for m in range(MATCH)]
    tiles = [(slice(c * CHUNK, (c + 1) * CHUNK), halves[b], b, None) for c, b in near]
    for m in range(MATCH):
        tiles.append((slice(NEAR + m * BLOCK, NEAR + (m + 1) * BLOCK), far_rows[m], None, m))
    for ref in (pb, dsb):
        ref[0:CHUNK, halves[1]] = jnp.zeros((CHUNK, BLOCK), BF16)
        ref[NEAR - CHUNK:NEAR, halves[0]] = jnp.zeros((CHUNK, BLOCK), BF16)
        ref[NEAR:KEYS, :] = jnp.zeros((MATCH * BLOCK, ROWS), BF16)

    def fold(value, how):
        return how(value.reshape(CHUNK // 8, 8, BLOCK), axis=0)

    def by_rows(near_parts, far_parts, how, none):
        joined = []
        for b in range(2):
            part = near_parts[b]
            for m in range(MATCH):
                part = how(part, jnp.where(picked[m] == b, far_parts[m], none))
            joined.append(part)
        return joined

    def of_tile(joined, b, m):
        return joined[b] if m is None else jnp.where(picked[m] == 0, joined[0], joined[1])

    def one_head(h, _):
        at = pl.ds(pl.multiple_of(h * HD, HD), HD)
        tops, far_tops = [jnp.full((8, BLOCK), -3e38, F32)] * 2, [None] * MATCH
        for c, r, b, m in tiles:
            s = tn(kt[at, c], qt[at, r])
            if m is None:
                s += bias[c, r]
                tops[b] = jnp.maximum(tops[b], fold(s, jnp.max))
            else:
                far_tops[m] = fold(s, jnp.max)
            s_ref[c, r] = s
        tops = [jnp.max(t, axis=0, keepdims=True) for t in by_rows(tops, far_tops, jnp.maximum, -3e38)]
        sums, far_sums = [jnp.zeros((8, BLOCK), F32)] * 2, [None] * MATCH
        inner, far_inner = [jnp.zeros((8, BLOCK), F32)] * 2, [None] * MATCH
        for c, r, b, m in tiles:
            e = jnp.exp2((s_ref[c, r] - of_tile(tops, b, m)) * (FACTOR * LOG2E))
            s_ref[c, r] = e
            dp = tn(vt[at, c], dt[at, r])
            dp_ref[c, r] = dp
            total, weighted = fold(e, jnp.sum), fold(e * dp, jnp.sum)
            if m is None:
                sums[b] += total
                inner[b] += weighted
            else:
                far_sums[m], far_inner[m] = total, weighted
        sums = by_rows(sums, far_sums, jnp.add, 0.0)
        inner = by_rows(inner, far_inner, jnp.add, 0.0)
        inverse = [1.0 / jnp.sum(t, axis=0, keepdims=True) for t in sums]
        mean = [jnp.sum(t, axis=0, keepdims=True) * i for t, i in zip(inner, inverse)]
        for c, r, b, m in tiles:
            p = s_ref[c, r] * of_tile(inverse, b, m)
            pb[c, r] = p.astype(BF16)
            dsb[c, r] = (p * (dp_ref[c, r] - of_tile(mean, b, m)) * FACTOR).astype(BF16)
        ot[at, :] = nn(vt[at, :], pb[...]).astype(BF16)
        dvt[at, :] = nt(dt[at, :], pb[...]).astype(BF16)
        dqt[at, :] = nn(kt[at, :], dsb[...]).astype(BF16)
        dkt[at, :] = nt(qt[at, :], dsb[...]).astype(BF16)
        return 0

    lax.fori_loop(0, HEADS, one_head, 0)

    mixed_ref[...] = tn(ot[...], wo_ref[...]).astype(BF16)
    ft[...] = nn(wk_ref[...], dkt[...]) + nn(wv_ref[...], dvt[...])
    f_own_ref[...] = (ft[:, own] + nn(wq_ref[...], dqt[...])).T
    for start, ref in zip(starts, (f_prev_ref, None, f_next_ref, f_far0_ref, f_far1_ref)):
        if ref is not None:
            ref[...] = ft[:, start:start + ref.shape[0]].astype(BF16).T
    scale = float(ROWS * 256) ** -0.5
    wg_ref[0:D, :] = (nt(xt[:, own], dqt[...]) * scale).astype(BF16)
    wg_ref[D:2 * D, :] = (nt(xt[...], dkt[...]) * scale).astype(BF16)
    wg_ref[2 * D:3 * D, :] = (nt(xt[...], dvt[...]) * scale).astype(BF16)
    wg_ref[3 * D:4 * D, :] = (nn(ot[...], cot_ref[...]) * scale).astype(BF16)


def attend(picks, reach, prev, own, following, far0, far1, cot, wq, wk, wv, wo):
    vmem = pl.BlockSpec(memory_space=pltpu.VMEM)
    smem = pl.BlockSpec(memory_space=pltpu.SMEM)
    shape = jax.ShapeDtypeStruct
    return pl.pallas_call(
        attend_kernel,
        out_shape=(
            shape((ROWS, D), BF16),
            shape((ROWS, D), F32),
            shape((HALF, D), BF16),
            shape((HALF, D), BF16),
            shape((BLOCK, D), BF16),
            shape((BLOCK, D), BF16),
            shape((4 * D, D), BF16),
        ),
        in_specs=[smem] + [vmem] * 11,
        out_specs=(vmem,) * 7,
        scratch_shapes=[
            pltpu.VMEM((D, KEYS), BF16),
            pltpu.VMEM((D, ROWS), BF16),
            pltpu.VMEM((D, ROWS), BF16),
            pltpu.VMEM((D, KEYS), BF16),
            pltpu.VMEM((D, KEYS), BF16),
            pltpu.VMEM((NEAR, ROWS), F32),
            pltpu.VMEM((KEYS, ROWS), F32),
            pltpu.VMEM((KEYS, ROWS), F32),
            pltpu.VMEM((KEYS, ROWS), BF16),
            pltpu.VMEM((KEYS, ROWS), BF16),
            pltpu.VMEM((D, ROWS), BF16),
            pltpu.VMEM((D, ROWS), BF16),
            pltpu.VMEM((D, KEYS), BF16),
            pltpu.VMEM((D, KEYS), BF16),
            pltpu.VMEM((D, KEYS), F32),
        ],
        compiler_params=pltpu.CompilerParams(vmem_limit_bytes=40 * 1024 * 1024),
        cost_estimate=pl.CostEstimate(
            flops=8_000_000_000, bytes_accessed=8_000_000, transcendentals=HEADS * KEYS * ROWS
        ),
    )(picks, reach, prev, own, following, far0, far1, cot, wq, wk, wv, wo)


def crossed(block, mask, digit):
    count = lax.axis_size(AXIS)
    bits = count.bit_length() - 1

    def move(offset):
        pairs = [(i, i ^ offset) for i in range(count)]
        return lambda piece: lax.ppermute(piece, AXIS, pairs) if offset else piece

    for low in range(0, bits, digit):
        value = (mask >> low) & ((1 << digit) - 1)
        block = lax.switch(value, [move(i << low) for i in range(1 << digit)], block)
    return block


def across(block, offset):
    return lax.ppermute(block, AXIS, [(i, i ^ offset) for i in range(lax.axis_size(AXIS))])


def tree(values):
    while len(values) > 1:
        values = [a + b for a, b in zip(values[::2], values[1::2])]
    return values[0]


def exchange(parts):
    low = GROUP // PLANE
    groups = [[i * LINE + j * low + k for i in range(PLANE) for k in range(low)] for j in range(LINE // low)]
    return lax.all_to_all(parts, AXIS, 0, 0, axis_index_groups=groups)


def summed(parts):
    low = GROUP // PLANE
    mine = tree([parts[i].astype(F32) for i in range(GROUP)]).astype(BF16)
    terms = [mine] + [across(mine, o * low) for o in range(1, LINE // low)]
    return tree([term.astype(F32) for term in terms]).astype(BF16)


def finish_kernel(picks_ref, own_ref, from_next_ref, from_prev_ref, far0_ref, far1_ref, total_ref, f_ref, wg_ref):
    far = [ref[...].astype(F32) for ref in (far0_ref, far1_ref)]
    for b in range(ROWS // BLOCK):
        span = slice(b * BLOCK, (b + 1) * BLOCK)
        value = own_ref[span, :] + from_next_ref[span, :].astype(F32) + from_prev_ref[span, :].astype(F32)
        for m in range(MATCH):
            value += jnp.where(picks_ref[0, m] == b, far[m], 0.0)
        f_ref[span, :] = value.astype(BF16)

    def widen(i, _):
        wg_ref[i] = total_ref[i].astype(F32)
        return 0

    lax.fori_loop(0, GROUP, widen, 0)


def finish(picks, own, from_next, from_prev, far0, far1, total):
    vmem = pl.BlockSpec(memory_space=pltpu.VMEM)
    smem = pl.BlockSpec(memory_space=pltpu.SMEM)
    shape = jax.ShapeDtypeStruct
    return pl.pallas_call(
        finish_kernel,
        out_shape=(shape((ROWS, D), BF16), shape((GROUP, PART, D), F32)),
        in_specs=[smem] + [vmem] * 6,
        out_specs=(vmem, vmem),
        compiler_params=pltpu.CompilerParams(vmem_limit_bytes=16 * 1024 * 1024),
    )(picks, own, from_next, from_prev, far0, far1, total)


def shards(features, w_query, w_key, w_value, w_out, cotangent, reach, picks, masks):
    count = lax.axis_size(AXIS)
    bits = count.bit_length() - 1
    up = [(i, (i + 1) % count) for i in range(count)]
    down = [(j, i) for i, j in up]
    picked = picks.reshape(1, MATCH)
    prev = lax.ppermute(features, AXIS, up)
    following = lax.ppermute(features, AXIS, down)
    halves = features.reshape(ROWS // BLOCK, BLOCK, D)
    outgoing = jnp.where(picks[:, :, None] == 0, halves[0][None], halves[1][None])
    both = jnp.sum(masks * jnp.array([1, count]))
    routes = [(both >> (m * bits)) & (count - 1) for m in range(MATCH)]
    far = [crossed(outgoing[m], routes[m], DIGIT) for m in range(MATCH)]
    mixed, f_own, f_prev, f_next, f_far0, f_far1, partial = attend(
        picked, reach, prev, features, following, far[0], far[1], cotangent,
        w_query, w_key, w_value, w_out,
    )
    parts = exchange(partial.reshape(GROUP, PART, D))
    from_next = lax.ppermute(f_prev, AXIS, down)
    from_prev = lax.ppermute(f_next, AXIS, up)
    far0 = crossed(f_far0, routes[0], DIGIT)
    parts, from_next, from_prev, far0 = lax.optimization_barrier((parts, from_next, from_prev, far0))
    copies = jnp.broadcast_to(summed(parts)[None], (GROUP, PART, D))
    copies, f_far1 = lax.optimization_barrier((copies, f_far1))
    total = exchange(copies)
    far1 = crossed(f_far1, routes[1], DIGIT)
    feature_grad, weight_grads = finish(picked, f_own, from_next, from_prev, far0, far1, total)
    return mixed, feature_grad, weight_grads.reshape(4, D, D)


def solution(mesh):
    return jax.shard_map(
        shards,
        mesh=mesh,
        in_specs=(
            P("blk", None),
            P(),
            P(),
            P(),
            P(),
            P("blk", None),
            P(None, "blk"),
            P(None, "blk"),
            P(),
        ),
        out_specs=(P("blk", None), P("blk", None), P()),
        check_vma=False,
    )
```

```python
import jax
import jax.numpy as jnp
from jax import lax
from jax.experimental import pallas as pl
from jax.experimental.pallas import tpu as pltpu
from jax.sharding import PartitionSpec as P

HEADS = 8
HALF = 256
BLOCK = 128
MATCH = 2
ROWS = 256
D = 384
HD = D // HEADS
NEAR = ROWS + 2 * HALF
KEYS = NEAR + MATCH * BLOCK
CHUNK = 128
FACTOR = HD ** -0.5
LOG2E = 1.4426950408889634
AXIS = "blk"
PLANE = 16
LINE = 16
GROUP = 64
PART = 4 * D // GROUP
DIGIT = 4
F32 = jnp.float32
BF16 = jnp.bfloat16


def nn(a, b):
    return lax.dot_general(a, b, (((1,), (0,)), ((), ())), preferred_element_type=F32)


def nt(a, b):
    return lax.dot_general(a, b, (((1,), (1,)), ((), ())), preferred_element_type=F32)


def tn(a, b):
    return lax.dot_general(a, b, (((0,), (0,)), ((), ())), preferred_element_type=F32)


def attend_kernel(
    picks_ref, reach_ref, prev_ref, own_ref, next_ref, far0_ref, far1_ref, cot_ref,
    wq_ref, wk_ref, wv_ref, wo_ref,
    mixed_ref, f_own_ref, f_prev_ref, f_next_ref, f_far0_ref, f_far1_ref, wg_ref,
    xt, qt, dt, kt, vt, bias, s_ref, dp_ref, pb, dsb, ot, dqt, dkt, dvt, ft,
):
    own = slice(HALF, HALF + ROWS)
    starts = (0, HALF, HALF + ROWS, NEAR, NEAR + BLOCK)
    for start, piece in zip(starts, (prev_ref, own_ref, next_ref, far0_ref, far1_ref)):
        xt[:, start:start + piece.shape[0]] = piece[...].T
    qt[...] = nn(wq_ref[...].T, xt[:, own]).astype(BF16)
    dt[...] = nt(wo_ref[...], cot_ref[...]).astype(BF16)
    kt[...] = nn(wk_ref[...].T, xt[...]).astype(BF16)
    vt[...] = nn(wv_ref[...].T, xt[...]).astype(BF16)

    rows = lax.broadcasted_iota(jnp.int32, (CHUNK, ROWS), 1)
    cols = lax.broadcasted_iota(jnp.int32, (CHUNK, ROWS), 0)
    offset = cols - HALF - rows
    back = -reach_ref[0:1, :]
    ahead = reach_ref[1:2, :]

    def near_bias(c, _):
        start = pl.multiple_of(c * CHUNK, CHUNK)
        allowed = (offset >= back - start) & (offset <= ahead - start)
        bias[pl.ds(start, CHUNK), :] = jnp.where(allowed, 0.0, -1e30)
        return 0

    lax.fori_loop(0, NEAR // CHUNK, near_bias, 0)

    halves = [slice(0, BLOCK), slice(BLOCK, ROWS)]
    near = [(c, b) for c in range(NEAR // CHUNK) for b in range(2) if b * BLOCK <= c * CHUNK <= b * BLOCK + 2 * HALF]
    picked = [picks_ref[0, m] for m in range(MATCH)]
    far_rows = [pl.ds(pl.multiple_of(picked[m] * BLOCK, BLOCK), BLOCK) for m in range(MATCH)]
    tiles = [(slice(c * CHUNK, (c + 1) * CHUNK), halves[b], b, None) for c, b in near]
    for m in range(MATCH):
        tiles.append((slice(NEAR + m * BLOCK, NEAR + (m + 1) * BLOCK), far_rows[m], None, m))
    for ref in (pb, dsb):
        ref[0:CHUNK, halves[1]] = jnp.zeros((CHUNK, BLOCK), BF16)
        ref[NEAR - CHUNK:NEAR, halves[0]] = jnp.zeros((CHUNK, BLOCK), BF16)
        ref[NEAR:KEYS, :] = jnp.zeros((MATCH * BLOCK, ROWS), BF16)

    def fold(value, how):
        return how(value.reshape(CHUNK // 8, 8, BLOCK), axis=0)

    def by_rows(near_parts, far_parts, how, none):
        joined = []
        for b in range(2):
            part = near_parts[b]
            for m in range(MATCH):
                part = how(part, jnp.where(picked[m] == b, far_parts[m], none))
            joined.append(part)
        return joined

    def of_tile(joined, b, m):
        return joined[b] if m is None else jnp.where(picked[m] == 0, joined[0], joined[1])

    def one_head(h, _):
        at = pl.ds(pl.multiple_of(h * HD, HD), HD)
        s_ref[...] = tn(kt[at, :], qt[at, :])
        dp_ref[...] = tn(vt[at, :], dt[at, :])
        tops, far_tops = [jnp.full((8, BLOCK), -3e38, F32)] * 2, [None] * MATCH
        for c, r, b, m in tiles:
            if m is None:
                tops[b] = jnp.maximum(tops[b], fold(s_ref[c, r] + bias[c, r], jnp.max))
            else:
                far_tops[m] = fold(s_ref[c, r], jnp.max)
        tops = [jnp.max(t, axis=0, keepdims=True) for t in by_rows(tops, far_tops, jnp.maximum, -3e38)]
        sums, far_sums = [jnp.zeros((8, BLOCK), F32)] * 2, [None] * MATCH
        inner, far_inner = [jnp.zeros((8, BLOCK), F32)] * 2, [None] * MATCH
        for c, r, b, m in tiles:
            s = s_ref[c, r] if m is not None else s_ref[c, r] + bias[c, r]
            e = jnp.exp2((s - of_tile(tops, b, m)) * (FACTOR * LOG2E))
            s_ref[c, r] = e
            total, weighted = fold(e, jnp.sum), fold(e * dp_ref[c, r], jnp.sum)
            if m is None:
                sums[b] += total
                inner[b] += weighted
            else:
                far_sums[m], far_inner[m] = total, weighted
        sums = by_rows(sums, far_sums, jnp.add, 0.0)
        inner = by_rows(inner, far_inner, jnp.add, 0.0)
        inverse = [1.0 / jnp.sum(t, axis=0, keepdims=True) for t in sums]
        mean = [jnp.sum(t, axis=0, keepdims=True) * i for t, i in zip(inner, inverse)]
        for c, r, b, m in tiles:
            p = s_ref[c, r] * of_tile(inverse, b, m)
            pb[c, r] = p.astype(BF16)
            dsb[c, r] = (p * (dp_ref[c, r] - of_tile(mean, b, m)) * FACTOR).astype(BF16)
        ot[at, :] = nn(vt[at, :], pb[...]).astype(BF16)
        dvt[at, :] = nt(dt[at, :], pb[...]).astype(BF16)
        dqt[at, :] = nn(kt[at, :], dsb[...]).astype(BF16)
        dkt[at, :] = nt(qt[at, :], dsb[...]).astype(BF16)
        return 0

    lax.fori_loop(0, HEADS, one_head, 0)

    mixed_ref[...] = tn(ot[...], wo_ref[...]).astype(BF16)
    ft[...] = nn(wk_ref[...], dkt[...]) + nn(wv_ref[...], dvt[...])
    f_own_ref[...] = (ft[:, own] + nn(wq_ref[...], dqt[...])).T
    for start, ref in zip(starts, (f_prev_ref, None, f_next_ref, f_far0_ref, f_far1_ref)):
        if ref is not None:
            ref[...] = ft[:, start:start + ref.shape[0]].astype(BF16).T
    scale = float(ROWS * 256) ** -0.5
    wg_ref[0:D, :] = (nt(xt[:, own], dqt[...]) * scale).astype(BF16)
    wg_ref[D:2 * D, :] = (nt(xt[...], dkt[...]) * scale).astype(BF16)
    wg_ref[2 * D:3 * D, :] = (nt(xt[...], dvt[...]) * scale).astype(BF16)
    wg_ref[3 * D:4 * D, :] = (nn(ot[...], cot_ref[...]) * scale).astype(BF16)


def attend(picks, reach, prev, own, following, far0, far1, cot, wq, wk, wv, wo):
    vmem = pl.BlockSpec(memory_space=pltpu.VMEM)
    smem = pl.BlockSpec(memory_space=pltpu.SMEM)
    shape = jax.ShapeDtypeStruct
    return pl.pallas_call(
        attend_kernel,
        out_shape=(
            shape((ROWS, D), BF16),
            shape((ROWS, D), F32),
            shape((HALF, D), BF16),
            shape((HALF, D), BF16),
            shape((BLOCK, D), BF16),
            shape((BLOCK, D), BF16),
            shape((4 * D, D), BF16),
        ),
        in_specs=[smem] + [vmem] * 11,
        out_specs=(vmem,) * 7,
        scratch_shapes=[
            pltpu.VMEM((D, KEYS), BF16),
            pltpu.VMEM((D, ROWS), BF16),
            pltpu.VMEM((D, ROWS), BF16),
            pltpu.VMEM((D, KEYS), BF16),
            pltpu.VMEM((D, KEYS), BF16),
            pltpu.VMEM((NEAR, ROWS), F32),
            pltpu.VMEM((KEYS, ROWS), F32),
            pltpu.VMEM((KEYS, ROWS), F32),
            pltpu.VMEM((KEYS, ROWS), BF16),
            pltpu.VMEM((KEYS, ROWS), BF16),
            pltpu.VMEM((D, ROWS), BF16),
            pltpu.VMEM((D, ROWS), BF16),
            pltpu.VMEM((D, KEYS), BF16),
            pltpu.VMEM((D, KEYS), BF16),
            pltpu.VMEM((D, KEYS), F32),
        ],
        compiler_params=pltpu.CompilerParams(vmem_limit_bytes=40 * 1024 * 1024),
        cost_estimate=pl.CostEstimate(
            flops=8_000_000_000, bytes_accessed=8_000_000, transcendentals=HEADS * KEYS * ROWS
        ),
    )(picks, reach, prev, own, following, far0, far1, cot, wq, wk, wv, wo)


def crossed(block, mask, digit):
    count = lax.axis_size(AXIS)
    bits = count.bit_length() - 1

    def move(offset):
        pairs = [(i, i ^ offset) for i in range(count)]
        return lambda piece: lax.ppermute(piece, AXIS, pairs) if offset else piece

    for low in range(0, bits, digit):
        value = (mask >> low) & ((1 << digit) - 1)
        block = lax.switch(value, [move(i << low) for i in range(1 << digit)], block)
    return block


def across(block, offset):
    return lax.ppermute(block, AXIS, [(i, i ^ offset) for i in range(lax.axis_size(AXIS))])


def tree(values):
    while len(values) > 1:
        values = [a + b for a, b in zip(values[::2], values[1::2])]
    return values[0]


def exchange(parts):
    low = GROUP // PLANE
    groups = [[i * LINE + j * low + k for i in range(PLANE) for k in range(low)] for j in range(LINE // low)]
    return lax.all_to_all(parts, AXIS, 0, 0, axis_index_groups=groups)


def summed(parts):
    low = GROUP // PLANE
    mine = tree([parts[i].astype(F32) for i in range(GROUP)]).astype(BF16)
    terms = [mine] + [across(mine, o * low) for o in range(1, LINE // low)]
    return tree([term.astype(F32) for term in terms]).astype(BF16)


def finish_kernel(picks_ref, own_ref, from_next_ref, from_prev_ref, far0_ref, far1_ref, total_ref, f_ref, wg_ref):
    wg_ref[...] = total_ref[...].astype(F32)

    @pl.when(pl.program_id(0) == 0)
    def _():
        far = [ref[...].astype(F32) for ref in (far0_ref, far1_ref)]
        for b in range(ROWS // BLOCK):
            span = slice(b * BLOCK, (b + 1) * BLOCK)
            value = own_ref[span, :] + from_next_ref[span, :].astype(F32) + from_prev_ref[span, :].astype(F32)
            for m in range(MATCH):
                value += jnp.where(picks_ref[0, m] == b, far[m], 0.0)
            f_ref[span, :] = value.astype(BF16)


def finish(picks, own, from_next, from_prev, far0, far1, total):
    vmem = pl.BlockSpec(memory_space=pltpu.VMEM)
    smem = pl.BlockSpec(memory_space=pltpu.SMEM)
    step = pl.BlockSpec((D, D), lambda i: (i, 0))
    shape = jax.ShapeDtypeStruct
    return pl.pallas_call(
        finish_kernel,
        grid=(4,),
        out_shape=(shape((ROWS, D), BF16), shape((4 * D, D), F32)),
        in_specs=[smem] + [vmem] * 5 + [step],
        out_specs=(vmem, step),
        compiler_params=pltpu.CompilerParams(vmem_limit_bytes=16 * 1024 * 1024),
    )(picks, own, from_next, from_prev, far0, far1, total.reshape(4 * D, D))


def shards(features, w_query, w_key, w_value, w_out, cotangent, reach, picks, masks):
    count = lax.axis_size(AXIS)
    bits = count.bit_length() - 1
    up = [(i, (i + 1) % count) for i in range(count)]
    down = [(j, i) for i, j in up]
    picked = picks.reshape(1, MATCH)
    halves = features.reshape(ROWS // BLOCK, BLOCK, D)
    outgoing = jnp.where(picks[:, :, None] == 0, halves[0][None], halves[1][None])
    both = jnp.sum(masks * jnp.array([1, count]))
    routes = [(both >> (m * bits)) & (count - 1) for m in range(MATCH)]
    far1 = crossed(outgoing[1], routes[1], DIGIT)
    edges, first, far1 = lax.optimization_barrier((features, outgoing[0], far1))
    prev = lax.ppermute(edges, AXIS, up)
    following = lax.ppermute(edges, AXIS, down)
    far0 = crossed(first, routes[0], DIGIT)
    mixed, f_own, f_prev, f_next, f_far0, f_far1, partial = attend(
        picked, reach, prev, features, following, far0, far1, cotangent,
        w_query, w_key, w_value, w_out,
    )
    parts = exchange(partial.reshape(GROUP, PART, D))
    from_next = lax.ppermute(f_prev, AXIS, down)
    from_prev = lax.ppermute(f_next, AXIS, up)
    far0 = crossed(f_far0, routes[0], DIGIT)
    parts, from_next, from_prev, far0 = lax.optimization_barrier((parts, from_next, from_prev, far0))
    copies = jnp.broadcast_to(summed(parts)[None], (GROUP, PART, D))
    copies, f_far1 = lax.optimization_barrier((copies, f_far1))
    total = exchange(copies)
    far1 = crossed(f_far1, routes[1], DIGIT)
    feature_grad, weight_grads = finish(picked, f_own, from_next, from_prev, far0, far1, total)
    return mixed, feature_grad, weight_grads.reshape(4, D, D)


def solution(mesh):
    return jax.shard_map(
        shards,
        mesh=mesh,
        in_specs=(
            P("blk", None),
            P(),
            P(),
            P(),
            P(),
            P("blk", None),
            P(None, "blk"),
            P(None, "blk"),
            P(),
        ),
        out_specs=(P("blk", None), P("blk", None), P()),
        check_vma=False,
    )
```

```python
import jax
import jax.numpy as jnp
from jax import lax
from jax.experimental import pallas as pl
from jax.experimental.pallas import tpu as pltpu
from jax.sharding import PartitionSpec as P

HEADS = 8
HALF = 256
BLOCK = 128
MATCH = 2
ROWS = 256
D = 384
HD = D // HEADS
NEAR = ROWS + 2 * HALF
KEYS = NEAR + MATCH * BLOCK
CHUNK = 128
FACTOR = HD ** -0.5
LOG2E = 1.4426950408889634
AXIS = "blk"
PLANE = 16
LINE = 16
GROUP = 64
PART = 4 * D // GROUP
DIGIT = 4
F32 = jnp.float32
BF16 = jnp.bfloat16


def nn(a, b):
    return lax.dot_general(a, b, (((1,), (0,)), ((), ())), preferred_element_type=F32)


def nt(a, b):
    return lax.dot_general(a, b, (((1,), (1,)), ((), ())), preferred_element_type=F32)


def tn(a, b):
    return lax.dot_general(a, b, (((0,), (0,)), ((), ())), preferred_element_type=F32)


def attend_kernel(
    picks_ref, reach_ref, prev_ref, own_ref, next_ref, far0_ref, far1_ref, cot_ref,
    wq_ref, wk_ref, wv_ref, wo_ref,
    mixed_ref, f_own_ref, f_prev_ref, f_next_ref, f_far0_ref, f_far1_ref, wg_ref,
    xt, qt, dt, kt, vt, bias, s_ref, dp_ref, pb, dsb, ot, dqt, dkt, dvt, ft,
):
    own = slice(HALF, HALF + ROWS)
    starts = (0, HALF, HALF + ROWS, NEAR, NEAR + BLOCK)
    for start, piece in zip(starts, (prev_ref, own_ref, next_ref, far0_ref, far1_ref)):
        xt[:, start:start + piece.shape[0]] = piece[...].T
    qt[...] = nn(wq_ref[...].T, xt[:, own]).astype(BF16)
    dt[...] = nt(wo_ref[...], cot_ref[...]).astype(BF16)
    kt[...] = nn(wk_ref[...].T, xt[...]).astype(BF16)
    vt[...] = nn(wv_ref[...].T, xt[...]).astype(BF16)

    rows = lax.broadcasted_iota(jnp.int32, (CHUNK, ROWS), 1)
    cols = lax.broadcasted_iota(jnp.int32, (CHUNK, ROWS), 0)
    offset = cols - HALF - rows
    back = -reach_ref[0:1, :]
    ahead = reach_ref[1:2, :]

    def near_bias(c, _):
        start = pl.multiple_of(c * CHUNK, CHUNK)
        allowed = (offset >= back - start) & (offset <= ahead - start)
        bias[pl.ds(start, CHUNK), :] = jnp.where(allowed, 0.0, -1e30)
        return 0

    lax.fori_loop(0, NEAR // CHUNK, near_bias, 0)

    halves = [slice(0, BLOCK), slice(BLOCK, ROWS)]
    near = [(c, b) for c in range(NEAR // CHUNK) for b in range(2) if b * BLOCK <= c * CHUNK <= b * BLOCK + 2 * HALF]
    picked = [picks_ref[0, m] for m in range(MATCH)]
    far_rows = [pl.ds(pl.multiple_of(picked[m] * BLOCK, BLOCK), BLOCK) for m in range(MATCH)]
    tiles = [(slice(c * CHUNK, (c + 1) * CHUNK), halves[b], b, None) for c, b in near]
    for m in range(MATCH):
        tiles.append((slice(NEAR + m * BLOCK, NEAR + (m + 1) * BLOCK), far_rows[m], None, m))
    for ref in (pb, dsb):
        ref[0:CHUNK, halves[1]] = jnp.zeros((CHUNK, BLOCK), BF16)
        ref[NEAR - CHUNK:NEAR, halves[0]] = jnp.zeros((CHUNK, BLOCK), BF16)
        ref[NEAR:KEYS, :] = jnp.zeros((MATCH * BLOCK, ROWS), BF16)

    def fold(value, how):
        return how(value.reshape(CHUNK // 8, 8, BLOCK), axis=0)

    def by_rows(near_parts, far_parts, how, none):
        joined = []
        for b in range(2):
            part = near_parts[b]
            for m in range(MATCH):
                part = how(part, jnp.where(picked[m] == b, far_parts[m], none))
            joined.append(part)
        return joined

    def of_tile(joined, b, m):
        return joined[b] if m is None else jnp.where(picked[m] == 0, joined[0], joined[1])

    def one_head(h, _):
        at = pl.ds(pl.multiple_of(h * HD, HD), HD)
        tops, far_tops = [jnp.full((8, BLOCK), -3e38, F32)] * 2, [None] * MATCH
        for c, r, b, m in tiles:
            s = tn(kt[at, c], qt[at, r])
            if m is None:
                s += bias[c, r]
                tops[b] = jnp.maximum(tops[b], fold(s, jnp.max))
            else:
                far_tops[m] = fold(s, jnp.max)
            s_ref[c, r] = s
        tops = [jnp.max(t, axis=0, keepdims=True) for t in by_rows(tops, far_tops, jnp.maximum, -3e38)]
        sums, far_sums = [jnp.zeros((8, BLOCK), F32)] * 2, [None] * MATCH
        inner, far_inner = [jnp.zeros((8, BLOCK), F32)] * 2, [None] * MATCH
        for c, r, b, m in tiles:
            e = jnp.exp2((s_ref[c, r] - of_tile(tops, b, m)) * (FACTOR * LOG2E))
            s_ref[c, r] = e
            dp = tn(vt[at, c], dt[at, r])
            dp_ref[c, r] = dp
            total, weighted = fold(e, jnp.sum), fold(e * dp, jnp.sum)
            if m is None:
                sums[b] += total
                inner[b] += weighted
            else:
                far_sums[m], far_inner[m] = total, weighted
        sums = by_rows(sums, far_sums, jnp.add, 0.0)
        inner = by_rows(inner, far_inner, jnp.add, 0.0)
        inverse = [1.0 / jnp.sum(t, axis=0, keepdims=True) for t in sums]
        mean = [jnp.sum(t, axis=0, keepdims=True) * i for t, i in zip(inner, inverse)]
        for c, r, b, m in tiles:
            p = s_ref[c, r] * of_tile(inverse, b, m)
            pb[c, r] = p.astype(BF16)
            dsb[c, r] = (p * (dp_ref[c, r] - of_tile(mean, b, m)) * FACTOR).astype(BF16)
        ot[at, :] = nn(vt[at, :], pb[...]).astype(BF16)
        dvt[at, :] = nt(dt[at, :], pb[...]).astype(BF16)
        dqt[at, :] = nn(kt[at, :], dsb[...]).astype(BF16)
        dkt[at, :] = nt(qt[at, :], dsb[...]).astype(BF16)
        return 0

    lax.fori_loop(0, HEADS, one_head, 0)

    mixed_ref[...] = tn(ot[...], wo_ref[...]).astype(BF16)
    ft[...] = nn(wk_ref[...], dkt[...]) + nn(wv_ref[...], dvt[...])
    f_own_ref[...] = (ft[:, own] + nn(wq_ref[...], dqt[...])).T
    for start, ref in zip(starts, (f_prev_ref, None, f_next_ref, f_far0_ref, f_far1_ref)):
        if ref is not None:
            ref[...] = ft[:, start:start + ref.shape[0]].astype(BF16).T
    scale = float(ROWS * 256) ** -0.5
    wg_ref[0:D, :] = (nt(xt[:, own], dqt[...]) * scale).astype(BF16)
    wg_ref[D:2 * D, :] = (nt(xt[...], dkt[...]) * scale).astype(BF16)
    wg_ref[2 * D:3 * D, :] = (nt(xt[...], dvt[...]) * scale).astype(BF16)
    wg_ref[3 * D:4 * D, :] = (nn(ot[...], cot_ref[...]) * scale).astype(BF16)


def attend(picks, reach, prev, own, following, far0, far1, cot, wq, wk, wv, wo):
    vmem = pl.BlockSpec(memory_space=pltpu.VMEM)
    smem = pl.BlockSpec(memory_space=pltpu.SMEM)
    shape = jax.ShapeDtypeStruct
    return pl.pallas_call(
        attend_kernel,
        out_shape=(
            shape((ROWS, D), BF16),
            shape((ROWS, D), F32),
            shape((HALF, D), BF16),
            shape((HALF, D), BF16),
            shape((BLOCK, D), BF16),
            shape((BLOCK, D), BF16),
            shape((4 * D, D), BF16),
        ),
        in_specs=[smem] + [vmem] * 11,
        out_specs=(vmem,) * 7,
        scratch_shapes=[
            pltpu.VMEM((D, KEYS), BF16),
            pltpu.VMEM((D, ROWS), BF16),
            pltpu.VMEM((D, ROWS), BF16),
            pltpu.VMEM((D, KEYS), BF16),
            pltpu.VMEM((D, KEYS), BF16),
            pltpu.VMEM((NEAR, ROWS), F32),
            pltpu.VMEM((KEYS, ROWS), F32),
            pltpu.VMEM((KEYS, ROWS), F32),
            pltpu.VMEM((KEYS, ROWS), BF16),
            pltpu.VMEM((KEYS, ROWS), BF16),
            pltpu.VMEM((D, ROWS), BF16),
            pltpu.VMEM((D, ROWS), BF16),
            pltpu.VMEM((D, KEYS), BF16),
            pltpu.VMEM((D, KEYS), BF16),
            pltpu.VMEM((D, KEYS), F32),
        ],
        compiler_params=pltpu.CompilerParams(vmem_limit_bytes=40 * 1024 * 1024),
        cost_estimate=pl.CostEstimate(
            flops=8_000_000_000, bytes_accessed=8_000_000, transcendentals=HEADS * KEYS * ROWS
        ),
    )(picks, reach, prev, own, following, far0, far1, cot, wq, wk, wv, wo)


def crossed(block, mask, digit):
    count = lax.axis_size(AXIS)
    bits = count.bit_length() - 1

    def move(offset):
        pairs = [(i, i ^ offset) for i in range(count)]
        return lambda piece: lax.ppermute(piece, AXIS, pairs) if offset else piece

    for low in range(0, bits, digit):
        value = (mask >> low) & ((1 << digit) - 1)
        block = lax.switch(value, [move(i << low) for i in range(1 << digit)], block)
    return block


def crossed_both(blocks, masks):
    bits = lax.axis_size(AXIS).bit_length() - 1

    def step(_, state):
        first, second, masks = state
        return second, crossed(first, masks & ((1 << bits) - 1), DIGIT), masks >> bits

    return lax.fori_loop(0, MATCH, step, (*blocks, masks))[:MATCH]


def across(block, offset):
    return lax.ppermute(block, AXIS, [(i, i ^ offset) for i in range(lax.axis_size(AXIS))])


def tree(values):
    while len(values) > 1:
        values = [a + b for a, b in zip(values[::2], values[1::2])]
    return values[0]


def exchange(parts):
    low = GROUP // PLANE
    groups = [[i * LINE + j * low + k for i in range(PLANE) for k in range(low)] for j in range(LINE // low)]
    return lax.all_to_all(parts, AXIS, 0, 0, axis_index_groups=groups)


def summed(parts):
    low = GROUP // PLANE
    mine = tree([parts[i].astype(F32) for i in range(GROUP)]).astype(BF16)
    terms = [mine] + [across(mine, o * low) for o in range(1, LINE // low)]
    return tree([term.astype(F32) for term in terms]).astype(BF16)


def finish_kernel(picks_ref, own_ref, from_next_ref, from_prev_ref, far0_ref, far1_ref, total_ref, f_ref, wg_ref):
    far = [ref[...].astype(F32) for ref in (far0_ref, far1_ref)]
    for b in range(ROWS // BLOCK):
        span = slice(b * BLOCK, (b + 1) * BLOCK)
        value = own_ref[span, :] + from_next_ref[span, :].astype(F32) + from_prev_ref[span, :].astype(F32)
        for m in range(MATCH):
            value += jnp.where(picks_ref[0, m] == b, far[m], 0.0)
        f_ref[span, :] = value.astype(BF16)

    def widen(i, _):
        wg_ref[i] = total_ref[i].astype(F32)
        return 0

    lax.fori_loop(0, GROUP, widen, 0)


def finish(picks, own, from_next, from_prev, far0, far1, total):
    vmem = pl.BlockSpec(memory_space=pltpu.VMEM)
    smem = pl.BlockSpec(memory_space=pltpu.SMEM)
    shape = jax.ShapeDtypeStruct
    return pl.pallas_call(
        finish_kernel,
        out_shape=(shape((ROWS, D), BF16), shape((GROUP, PART, D), F32)),
        in_specs=[smem] + [vmem] * 6,
        out_specs=(vmem, vmem),
        compiler_params=pltpu.CompilerParams(vmem_limit_bytes=16 * 1024 * 1024),
    )(picks, own, from_next, from_prev, far0, far1, total)


def shards(features, w_query, w_key, w_value, w_out, cotangent, reach, picks, masks):
    count = lax.axis_size(AXIS)
    bits = count.bit_length() - 1
    up = [(i, (i + 1) % count) for i in range(count)]
    down = [(j, i) for i, j in up]
    picked = picks.reshape(1, MATCH)
    prev = lax.ppermute(features, AXIS, up)
    following = lax.ppermute(features, AXIS, down)
    halves = features.reshape(ROWS // BLOCK, BLOCK, D)
    outgoing = jnp.where(picks[:, :, None] == 0, halves[0][None], halves[1][None])
    both = jnp.sum(masks * jnp.array([1, count]))
    routes = [(both >> (m * bits)) & (count - 1) for m in range(MATCH)]
    far = crossed_both((outgoing[0], outgoing[1]), both)
    mixed, f_own, f_prev, f_next, f_far0, f_far1, partial = attend(
        picked, reach, prev, features, following, far[0], far[1], cotangent,
        w_query, w_key, w_value, w_out,
    )
    parts = exchange(partial.reshape(GROUP, PART, D))
    from_next = lax.ppermute(f_prev, AXIS, down)
    from_prev = lax.ppermute(f_next, AXIS, up)
    far0 = crossed(f_far0, routes[0], DIGIT)
    parts, from_next, from_prev, far0 = lax.optimization_barrier((parts, from_next, from_prev, far0))
    copies = jnp.broadcast_to(summed(parts)[None], (GROUP, PART, D))
    copies, f_far1 = lax.optimization_barrier((copies, f_far1))
    total = exchange(copies)
    far1 = crossed(f_far1, routes[1], DIGIT)
    feature_grad, weight_grads = finish(picked, f_own, from_next, from_prev, far0, far1, total)
    return mixed, feature_grad, weight_grads.reshape(4, D, D)


def solution(mesh):
    return jax.shard_map(
        shards,
        mesh=mesh,
        in_specs=(
            P("blk", None),
            P(),
            P(),
            P(),
            P(),
            P("blk", None),
            P(None, "blk"),
            P(None, "blk"),
            P(),
        ),
        out_specs=(P("blk", None), P("blk", None), P()),
        check_vma=False,
    )
```

```python
import jax
import jax.numpy as jnp
from jax import lax
from jax.experimental import pallas as pl
from jax.experimental.pallas import tpu as pltpu
from jax.sharding import PartitionSpec as P

HEADS = 8
HALF = 256
BLOCK = 128
MATCH = 2
ROWS = 256
D = 384
HD = D // HEADS
NEAR = ROWS + 2 * HALF
KEYS = NEAR + MATCH * BLOCK
CHUNK = 128
FACTOR = HD ** -0.5
LOG2E = 1.4426950408889634
AXIS = "blk"
PLANE = 16
LINE = 16
GROUP = 32
PART = 4 * D // GROUP
DIGIT = 4
F32 = jnp.float32
BF16 = jnp.bfloat16


def nn(a, b):
    return lax.dot_general(a, b, (((1,), (0,)), ((), ())), preferred_element_type=F32)


def nt(a, b):
    return lax.dot_general(a, b, (((1,), (1,)), ((), ())), preferred_element_type=F32)


def tn(a, b):
    return lax.dot_general(a, b, (((0,), (0,)), ((), ())), preferred_element_type=F32)


def attend_kernel(
    picks_ref, reach_ref, prev_ref, own_ref, next_ref, far0_ref, far1_ref, cot_ref,
    wq_ref, wk_ref, wv_ref, wo_ref,
    mixed_ref, f_own_ref, f_prev_ref, f_next_ref, f_far0_ref, f_far1_ref, wg_ref,
    xt, qt, dt, kt, vt, bias, s_ref, dp_ref, pb, dsb, ot, dqt, dkt, dvt, ft,
):
    own = slice(HALF, HALF + ROWS)
    starts = (0, HALF, HALF + ROWS, NEAR, NEAR + BLOCK)
    for start, piece in zip(starts, (prev_ref, own_ref, next_ref, far0_ref, far1_ref)):
        xt[:, start:start + piece.shape[0]] = piece[...].T
    qt[...] = nn(wq_ref[...].T, xt[:, own]).astype(BF16)
    dt[...] = nt(wo_ref[...], cot_ref[...]).astype(BF16)
    kt[...] = nn(wk_ref[...].T, xt[...]).astype(BF16)
    vt[...] = nn(wv_ref[...].T, xt[...]).astype(BF16)

    rows = lax.broadcasted_iota(jnp.int32, (CHUNK, ROWS), 1)
    cols = lax.broadcasted_iota(jnp.int32, (CHUNK, ROWS), 0)
    offset = cols - HALF - rows
    back = -reach_ref[0:1, :]
    ahead = reach_ref[1:2, :]

    def near_bias(c, _):
        start = pl.multiple_of(c * CHUNK, CHUNK)
        allowed = (offset >= back - start) & (offset <= ahead - start)
        bias[pl.ds(start, CHUNK), :] = jnp.where(allowed, 0.0, -1e30)
        return 0

    lax.fori_loop(0, NEAR // CHUNK, near_bias, 0)

    halves = [slice(0, BLOCK), slice(BLOCK, ROWS)]
    near = [(c, b) for c in range(NEAR // CHUNK) for b in range(2) if b * BLOCK <= c * CHUNK <= b * BLOCK + 2 * HALF]
    picked = [picks_ref[0, m] for m in range(MATCH)]
    far_rows = [pl.ds(pl.multiple_of(picked[m] * BLOCK, BLOCK), BLOCK) for m in range(MATCH)]
    tiles = [(slice(c * CHUNK, (c + 1) * CHUNK), halves[b], b, None) for c, b in near]
    for m in range(MATCH):
        tiles.append((slice(NEAR + m * BLOCK, NEAR + (m + 1) * BLOCK), far_rows[m], None, m))
    for ref in (pb, dsb):
        ref[0:CHUNK, halves[1]] = jnp.zeros((CHUNK, BLOCK), BF16)
        ref[NEAR - CHUNK:NEAR, halves[0]] = jnp.zeros((CHUNK, BLOCK), BF16)
        ref[NEAR:KEYS, :] = jnp.zeros((MATCH * BLOCK, ROWS), BF16)

    def fold(value, how):
        return how(value.reshape(CHUNK // 8, 8, BLOCK), axis=0)

    def by_rows(near_parts, far_parts, how, none):
        joined = []
        for b in range(2):
            part = near_parts[b]
            for m in range(MATCH):
                part = how(part, jnp.where(picked[m] == b, far_parts[m], none))
            joined.append(part)
        return joined

    def of_tile(joined, b, m):
        return joined[b] if m is None else jnp.where(picked[m] == 0, joined[0], joined[1])

    def one_head(h, _):
        at = pl.ds(pl.multiple_of(h * HD, HD), HD)
        tops, far_tops = [jnp.full((8, BLOCK), -3e38, F32)] * 2, [None] * MATCH
        for c, r, b, m in tiles:
            s = tn(kt[at, c], qt[at, r])
            if m is None:
                s += bias[c, r]
                tops[b] = jnp.maximum(tops[b], fold(s, jnp.max))
            else:
                far_tops[m] = fold(s, jnp.max)
            s_ref[c, r] = s
        tops = [jnp.max(t, axis=0, keepdims=True) for t in by_rows(tops, far_tops, jnp.maximum, -3e38)]
        sums, far_sums = [jnp.zeros((8, BLOCK), F32)] * 2, [None] * MATCH
        inner, far_inner = [jnp.zeros((8, BLOCK), F32)] * 2, [None] * MATCH
        for c, r, b, m in tiles:
            e = jnp.exp2((s_ref[c, r] - of_tile(tops, b, m)) * (FACTOR * LOG2E))
            s_ref[c, r] = e
            dp = tn(vt[at, c], dt[at, r])
            dp_ref[c, r] = dp
            total, weighted = fold(e, jnp.sum), fold(e * dp, jnp.sum)
            if m is None:
                sums[b] += total
                inner[b] += weighted
            else:
                far_sums[m], far_inner[m] = total, weighted
        sums = by_rows(sums, far_sums, jnp.add, 0.0)
        inner = by_rows(inner, far_inner, jnp.add, 0.0)
        inverse = [1.0 / jnp.sum(t, axis=0, keepdims=True) for t in sums]
        mean = [jnp.sum(t, axis=0, keepdims=True) * i for t, i in zip(inner, inverse)]
        for c, r, b, m in tiles:
            p = s_ref[c, r] * of_tile(inverse, b, m)
            pb[c, r] = p.astype(BF16)
            dsb[c, r] = (p * (dp_ref[c, r] - of_tile(mean, b, m)) * FACTOR).astype(BF16)
        ot[at, :] = nn(vt[at, :], pb[...]).astype(BF16)
        dvt[at, :] = nt(dt[at, :], pb[...]).astype(BF16)
        dqt[at, :] = nn(kt[at, :], dsb[...]).astype(BF16)
        dkt[at, :] = nt(qt[at, :], dsb[...]).astype(BF16)
        return 0

    lax.fori_loop(0, HEADS, one_head, 0)

    mixed_ref[...] = tn(ot[...], wo_ref[...]).astype(BF16)
    ft[...] = nn(wk_ref[...], dkt[...]) + nn(wv_ref[...], dvt[...])
    f_own_ref[...] = (ft[:, own] + nn(wq_ref[...], dqt[...])).T
    for start, ref in zip(starts, (f_prev_ref, None, f_next_ref, f_far0_ref, f_far1_ref)):
        if ref is not None:
            ref[...] = ft[:, start:start + ref.shape[0]].astype(BF16).T
    scale = float(ROWS * 256) ** -0.5
    wg_ref[0:D, :] = (nt(xt[:, own], dqt[...]) * scale).astype(BF16)
    wg_ref[D:2 * D, :] = (nt(xt[...], dkt[...]) * scale).astype(BF16)
    wg_ref[2 * D:3 * D, :] = (nt(xt[...], dvt[...]) * scale).astype(BF16)
    wg_ref[3 * D:4 * D, :] = (nn(ot[...], cot_ref[...]) * scale).astype(BF16)


def attend(picks, reach, prev, own, following, far0, far1, cot, wq, wk, wv, wo):
    vmem = pl.BlockSpec(memory_space=pltpu.VMEM)
    smem = pl.BlockSpec(memory_space=pltpu.SMEM)
    shape = jax.ShapeDtypeStruct
    return pl.pallas_call(
        attend_kernel,
        out_shape=(
            shape((ROWS, D), BF16),
            shape((ROWS, D), F32),
            shape((HALF, D), BF16),
            shape((HALF, D), BF16),
            shape((BLOCK, D), BF16),
            shape((BLOCK, D), BF16),
            shape((4 * D, D), BF16),
        ),
        in_specs=[smem] + [vmem] * 11,
        out_specs=(vmem,) * 7,
        scratch_shapes=[
            pltpu.VMEM((D, KEYS), BF16),
            pltpu.VMEM((D, ROWS), BF16),
            pltpu.VMEM((D, ROWS), BF16),
            pltpu.VMEM((D, KEYS), BF16),
            pltpu.VMEM((D, KEYS), BF16),
            pltpu.VMEM((NEAR, ROWS), F32),
            pltpu.VMEM((KEYS, ROWS), F32),
            pltpu.VMEM((KEYS, ROWS), F32),
            pltpu.VMEM((KEYS, ROWS), BF16),
            pltpu.VMEM((KEYS, ROWS), BF16),
            pltpu.VMEM((D, ROWS), BF16),
            pltpu.VMEM((D, ROWS), BF16),
            pltpu.VMEM((D, KEYS), BF16),
            pltpu.VMEM((D, KEYS), BF16),
            pltpu.VMEM((D, KEYS), F32),
        ],
        compiler_params=pltpu.CompilerParams(vmem_limit_bytes=40 * 1024 * 1024),
        cost_estimate=pl.CostEstimate(
            flops=8_000_000_000, bytes_accessed=8_000_000, transcendentals=HEADS * KEYS * ROWS
        ),
    )(picks, reach, prev, own, following, far0, far1, cot, wq, wk, wv, wo)


def crossed(block, mask, digit):
    count = lax.axis_size(AXIS)
    bits = count.bit_length() - 1

    def move(offset):
        pairs = [(i, i ^ offset) for i in range(count)]
        return lambda piece: lax.ppermute(piece, AXIS, pairs) if offset else piece

    for low in range(0, bits, digit):
        value = (mask >> low) & ((1 << digit) - 1)
        block = lax.switch(value, [move(i << low) for i in range(1 << digit)], block)
    return block


def crossed_both(blocks, masks):
    bits = lax.axis_size(AXIS).bit_length() - 1

    def step(_, state):
        first, second, masks = state
        return second, crossed(first, masks & ((1 << bits) - 1), DIGIT), masks >> bits

    return lax.fori_loop(0, MATCH, step, (*blocks, masks))[:MATCH]


def across(block, offset):
    return lax.ppermute(block, AXIS, [(i, i ^ offset) for i in range(lax.axis_size(AXIS))])


def tree(values):
    while len(values) > 1:
        values = [a + b for a, b in zip(values[::2], values[1::2])]
    return values[0]


def exchange(parts):
    low = GROUP // PLANE
    groups = [[i * LINE + j * low + k for i in range(PLANE) for k in range(low)] for j in range(LINE // low)]
    return lax.all_to_all(parts, AXIS, 0, 0, axis_index_groups=groups)


def summed(parts):
    low = GROUP // PLANE
    mine = tree([parts[i].astype(F32) for i in range(GROUP)]).astype(BF16)
    for step, ways in ((low, 4), (4 * low, LINE // (4 * low))):
        terms = [mine] + [across(mine, o * step) for o in range(1, ways)]
        mine = tree([term.astype(F32) for term in terms]).astype(BF16)
    return mine


def finish_kernel(picks_ref, own_ref, from_next_ref, from_prev_ref, far0_ref, far1_ref, total_ref, f_ref, wg_ref):
    far = [ref[...].astype(F32) for ref in (far0_ref, far1_ref)]
    for b in range(ROWS // BLOCK):
        span = slice(b * BLOCK, (b + 1) * BLOCK)
        value = own_ref[span, :] + from_next_ref[span, :].astype(F32) + from_prev_ref[span, :].astype(F32)
        for m in range(MATCH):
            value += jnp.where(picks_ref[0, m] == b, far[m], 0.0)
        f_ref[span, :] = value.astype(BF16)

    def widen(i, _):
        wg_ref[i] = total_ref[i].astype(F32)
        return 0

    lax.fori_loop(0, GROUP, widen, 0)


def finish(picks, own, from_next, from_prev, far0, far1, total):
    vmem = pl.BlockSpec(memory_space=pltpu.VMEM)
    smem = pl.BlockSpec(memory_space=pltpu.SMEM)
    shape = jax.ShapeDtypeStruct
    return pl.pallas_call(
        finish_kernel,
        out_shape=(shape((ROWS, D), BF16), shape((GROUP, PART, D), F32)),
        in_specs=[smem] + [vmem] * 6,
        out_specs=(vmem, vmem),
        compiler_params=pltpu.CompilerParams(vmem_limit_bytes=16 * 1024 * 1024),
    )(picks, own, from_next, from_prev, far0, far1, total)


def shards(features, w_query, w_key, w_value, w_out, cotangent, reach, picks, masks):
    count = lax.axis_size(AXIS)
    bits = count.bit_length() - 1
    up = [(i, (i + 1) % count) for i in range(count)]
    down = [(j, i) for i, j in up]
    picked = picks.reshape(1, MATCH)
    prev = lax.ppermute(features, AXIS, up)
    following = lax.ppermute(features, AXIS, down)
    halves = features.reshape(ROWS // BLOCK, BLOCK, D)
    outgoing = jnp.where(picks[:, :, None] == 0, halves[0][None], halves[1][None])
    both = jnp.sum(masks * jnp.array([1, count]))
    routes = [(both >> (m * bits)) & (count - 1) for m in range(MATCH)]
    far = crossed_both((outgoing[0], outgoing[1]), both)
    mixed, f_own, f_prev, f_next, f_far0, f_far1, partial = attend(
        picked, reach, prev, features, following, far[0], far[1], cotangent,
        w_query, w_key, w_value, w_out,
    )
    parts = exchange(partial.reshape(GROUP, PART, D))
    from_next = lax.ppermute(f_prev, AXIS, down)
    from_prev = lax.ppermute(f_next, AXIS, up)
    far0 = crossed(f_far0, routes[0], DIGIT)
    parts, from_next, from_prev, far0 = lax.optimization_barrier((parts, from_next, from_prev, far0))
    copies = jnp.broadcast_to(summed(parts)[None], (GROUP, PART, D))
    copies, f_far1 = lax.optimization_barrier((copies, f_far1))
    total = exchange(copies)
    far1 = crossed(f_far1, routes[1], DIGIT)
    feature_grad, weight_grads = finish(picked, f_own, from_next, from_prev, far0, far1, total)
    return mixed, feature_grad, weight_grads.reshape(4, D, D)


def solution(mesh):
    return jax.shard_map(
        shards,
        mesh=mesh,
        in_specs=(
            P("blk", None),
            P(),
            P(),
            P(),
            P(),
            P("blk", None),
            P(None, "blk"),
            P(None, "blk"),
            P(),
        ),
        out_specs=(P("blk", None), P("blk", None), P()),
        check_vma=False,
    )
```

```python
import jax
import jax.numpy as jnp
from jax import lax
from jax.experimental import pallas as pl
from jax.experimental.pallas import tpu as pltpu
from jax.sharding import PartitionSpec as P

HEADS = 8
HALF = 256
BLOCK = 128
MATCH = 2
ROWS = 256
D = 384
HD = D // HEADS
NEAR = ROWS + 2 * HALF
KEYS = NEAR + MATCH * BLOCK
CHUNK = 128
FACTOR = HD ** -0.5
LOG2E = 1.4426950408889634
AXIS = "blk"
PLANE = 16
LINE = 16
GROUP = 32
PART = 4 * D // GROUP
DIGIT = 4
F32 = jnp.float32
BF16 = jnp.bfloat16


def nn(a, b):
    return lax.dot_general(a, b, (((1,), (0,)), ((), ())), preferred_element_type=F32)


def nt(a, b):
    return lax.dot_general(a, b, (((1,), (1,)), ((), ())), preferred_element_type=F32)


def tn(a, b):
    return lax.dot_general(a, b, (((0,), (0,)), ((), ())), preferred_element_type=F32)


def attend_kernel(
    picks_ref, reach_ref, prev_ref, own_ref, next_ref, far0_ref, far1_ref, cot_ref,
    wq_ref, wk_ref, wv_ref, wo_ref,
    mixed_ref, f_own_ref, f_prev_ref, f_next_ref, f_far0_ref, f_far1_ref, wg_ref,
    xt, qt, dt, kt, vt, bias, s_ref, dp_ref, pb, dsb, ot, dqt, dkt, dvt, ft,
):
    own = slice(HALF, HALF + ROWS)
    starts = (0, HALF, HALF + ROWS, NEAR, NEAR + BLOCK)
    for start, piece in zip(starts, (prev_ref, own_ref, next_ref, far0_ref, far1_ref)):
        xt[:, start:start + piece.shape[0]] = piece[...].T
    qt[...] = nn(wq_ref[...].T, xt[:, own]).astype(BF16)
    dt[...] = nt(wo_ref[...], cot_ref[...]).astype(BF16)
    kt[...] = nn(wk_ref[...].T, xt[...]).astype(BF16)
    vt[...] = nn(wv_ref[...].T, xt[...]).astype(BF16)

    rows = lax.broadcasted_iota(jnp.int32, (CHUNK, ROWS), 1)
    cols = lax.broadcasted_iota(jnp.int32, (CHUNK, ROWS), 0)
    offset = cols - HALF - rows
    back = -reach_ref[0:1, :]
    ahead = reach_ref[1:2, :]

    def near_bias(c, _):
        start = pl.multiple_of(c * CHUNK, CHUNK)
        allowed = (offset >= back - start) & (offset <= ahead - start)
        bias[pl.ds(start, CHUNK), :] = jnp.where(allowed, 0.0, -1e30)
        return 0

    lax.fori_loop(0, NEAR // CHUNK, near_bias, 0)

    halves = [slice(0, BLOCK), slice(BLOCK, ROWS)]
    near = [(c, b) for c in range(NEAR // CHUNK) for b in range(2) if b * BLOCK <= c * CHUNK <= b * BLOCK + 2 * HALF]
    picked = [picks_ref[0, m] for m in range(MATCH)]
    far_rows = [pl.ds(pl.multiple_of(picked[m] * BLOCK, BLOCK), BLOCK) for m in range(MATCH)]
    tiles = [(slice(c * CHUNK, (c + 1) * CHUNK), halves[b], b, None) for c, b in near]
    for m in range(MATCH):
        tiles.append((slice(NEAR + m * BLOCK, NEAR + (m + 1) * BLOCK), far_rows[m], None, m))
    for ref in (pb, dsb):
        ref[0:CHUNK, halves[1]] = jnp.zeros((CHUNK, BLOCK), BF16)
        ref[NEAR - CHUNK:NEAR, halves[0]] = jnp.zeros((CHUNK, BLOCK), BF16)
        ref[NEAR:KEYS, :] = jnp.zeros((MATCH * BLOCK, ROWS), BF16)

    def fold(value, how):
        return how(value.reshape(CHUNK // 8, 8, BLOCK), axis=0)

    def by_rows(near_parts, far_parts, how, none):
        joined = []
        for b in range(2):
            part = near_parts[b]
            for m in range(MATCH):
                part = how(part, jnp.where(picked[m] == b, far_parts[m], none))
            joined.append(part)
        return joined

    def of_tile(joined, b, m):
        return joined[b] if m is None else jnp.where(picked[m] == 0, joined[0], joined[1])

    def one_head(h, _):
        at = pl.ds(pl.multiple_of(h * HD, HD), HD)
        tops, far_tops = [jnp.full((8, BLOCK), -3e38, F32)] * 2, [None] * MATCH
        for c, r, b, m in tiles:
            s = tn(kt[at, c], qt[at, r])
            if m is None:
                s += bias[c, r]
                tops[b] = jnp.maximum(tops[b], fold(s, jnp.max))
            else:
                far_tops[m] = fold(s, jnp.max)
            s_ref[c, r] = s
        tops = [jnp.max(t, axis=0, keepdims=True) for t in by_rows(tops, far_tops, jnp.maximum, -3e38)]
        sums, far_sums = [jnp.zeros((8, BLOCK), F32)] * 2, [None] * MATCH
        inner, far_inner = [jnp.zeros((8, BLOCK), F32)] * 2, [None] * MATCH
        for c, r, b, m in tiles:
            e = jnp.exp2((s_ref[c, r] - of_tile(tops, b, m)) * (FACTOR * LOG2E))
            s_ref[c, r] = e
            dp = tn(vt[at, c], dt[at, r])
            dp_ref[c, r] = dp
            total, weighted = fold(e, jnp.sum), fold(e * dp, jnp.sum)
            if m is None:
                sums[b] += total
                inner[b] += weighted
            else:
                far_sums[m], far_inner[m] = total, weighted
        sums = by_rows(sums, far_sums, jnp.add, 0.0)
        inner = by_rows(inner, far_inner, jnp.add, 0.0)
        inverse = [1.0 / jnp.sum(t, axis=0, keepdims=True) for t in sums]
        mean = [jnp.sum(t, axis=0, keepdims=True) * i for t, i in zip(inner, inverse)]
        for c, r, b, m in tiles:
            p = s_ref[c, r] * of_tile(inverse, b, m)
            pb[c, r] = p.astype(BF16)
            dsb[c, r] = (p * (dp_ref[c, r] - of_tile(mean, b, m)) * FACTOR).astype(BF16)
        ot[at, :] = nn(vt[at, :], pb[...]).astype(BF16)
        dvt[at, :] = nt(dt[at, :], pb[...]).astype(BF16)
        dqt[at, :] = nn(kt[at, :], dsb[...]).astype(BF16)
        dkt[at, :] = nt(qt[at, :], dsb[...]).astype(BF16)
        return 0

    lax.fori_loop(0, HEADS, one_head, 0)

    mixed_ref[...] = tn(ot[...], wo_ref[...]).astype(BF16)
    ft[...] = nn(wk_ref[...], dkt[...]) + nn(wv_ref[...], dvt[...])
    f_own_ref[...] = (ft[:, own] + nn(wq_ref[...], dqt[...])).T
    for start, ref in zip(starts, (f_prev_ref, None, f_next_ref, f_far0_ref, f_far1_ref)):
        if ref is not None:
            ref[...] = ft[:, start:start + ref.shape[0]].astype(BF16).T
    scale = float(ROWS * 256) ** -0.5
    wg_ref[0:D, :] = (nt(xt[:, own], dqt[...]) * scale).astype(BF16)
    wg_ref[D:2 * D, :] = (nt(xt[...], dkt[...]) * scale).astype(BF16)
    wg_ref[2 * D:3 * D, :] = (nt(xt[...], dvt[...]) * scale).astype(BF16)
    wg_ref[3 * D:4 * D, :] = (nn(ot[...], cot_ref[...]) * scale).astype(BF16)


def attend(picks, reach, prev, own, following, far0, far1, cot, wq, wk, wv, wo):
    vmem = pl.BlockSpec(memory_space=pltpu.VMEM)
    smem = pl.BlockSpec(memory_space=pltpu.SMEM)
    shape = jax.ShapeDtypeStruct
    return pl.pallas_call(
        attend_kernel,
        out_shape=(
            shape((ROWS, D), BF16),
            shape((ROWS, D), F32),
            shape((HALF, D), BF16),
            shape((HALF, D), BF16),
            shape((BLOCK, D), BF16),
            shape((BLOCK, D), BF16),
            shape((4 * D, D), BF16),
        ),
        in_specs=[smem] + [vmem] * 11,
        out_specs=(vmem,) * 7,
        scratch_shapes=[
            pltpu.VMEM((D, KEYS), BF16),
            pltpu.VMEM((D, ROWS), BF16),
            pltpu.VMEM((D, ROWS), BF16),
            pltpu.VMEM((D, KEYS), BF16),
            pltpu.VMEM((D, KEYS), BF16),
            pltpu.VMEM((NEAR, ROWS), F32),
            pltpu.VMEM((KEYS, ROWS), F32),
            pltpu.VMEM((KEYS, ROWS), F32),
            pltpu.VMEM((KEYS, ROWS), BF16),
            pltpu.VMEM((KEYS, ROWS), BF16),
            pltpu.VMEM((D, ROWS), BF16),
            pltpu.VMEM((D, ROWS), BF16),
            pltpu.VMEM((D, KEYS), BF16),
            pltpu.VMEM((D, KEYS), BF16),
            pltpu.VMEM((D, KEYS), F32),
        ],
        compiler_params=pltpu.CompilerParams(vmem_limit_bytes=40 * 1024 * 1024),
        cost_estimate=pl.CostEstimate(
            flops=8_000_000_000, bytes_accessed=8_000_000, transcendentals=HEADS * KEYS * ROWS
        ),
    )(picks, reach, prev, own, following, far0, far1, cot, wq, wk, wv, wo)


def crossed(block, mask, digit):
    count = lax.axis_size(AXIS)
    bits = count.bit_length() - 1

    def move(offset):
        pairs = [(i, i ^ offset) for i in range(count)]
        return lambda piece: lax.ppermute(piece, AXIS, pairs) if offset else piece

    for low in range(0, bits, digit):
        value = (mask >> low) & ((1 << digit) - 1)
        block = lax.switch(value, [move(i << low) for i in range(1 << digit)], block)
    return block


def crossed_both(blocks, masks):
    bits = lax.axis_size(AXIS).bit_length() - 1

    def step(_, state):
        first, second, masks = state
        return second, crossed(first, masks & ((1 << bits) - 1), DIGIT), masks >> bits

    return lax.fori_loop(0, MATCH, step, (*blocks, masks))[:MATCH]


def across(block, offset):
    return lax.ppermute(block, AXIS, [(i, i ^ offset) for i in range(lax.axis_size(AXIS))])


def tree(values):
    while len(values) > 1:
        values = [a + b for a, b in zip(values[::2], values[1::2])]
    return values[0]


def exchange(parts):
    low = GROUP // PLANE
    groups = [[i * LINE + j * low + k for i in range(PLANE) for k in range(low)] for j in range(LINE // low)]
    return lax.all_to_all(parts, AXIS, 0, 0, axis_index_groups=groups)


def summed(mine):
    low = GROUP // PLANE
    for step, ways in ((low, 4), (4 * low, LINE // (4 * low))):
        terms = [mine] + [across(mine, o * step) for o in range(1, ways)]
        mine = tree([term.astype(F32) for term in terms]).astype(BF16)
    return mine


def finish_kernel(picks_ref, own_ref, from_next_ref, from_prev_ref, far0_ref, far1_ref, total_ref, f_ref, wg_ref):
    far = [ref[...].astype(F32) for ref in (far0_ref, far1_ref)]
    for b in range(ROWS // BLOCK):
        span = slice(b * BLOCK, (b + 1) * BLOCK)
        value = own_ref[span, :] + from_next_ref[span, :].astype(F32) + from_prev_ref[span, :].astype(F32)
        for m in range(MATCH):
            value += jnp.where(picks_ref[0, m] == b, far[m], 0.0)
        f_ref[span, :] = value.astype(BF16)

    def widen(i, _):
        wg_ref[i] = total_ref[i].astype(F32)
        return 0

    lax.fori_loop(0, GROUP, widen, 0)


def finish(picks, own, from_next, from_prev, far0, far1, total):
    vmem = pl.BlockSpec(memory_space=pltpu.VMEM)
    smem = pl.BlockSpec(memory_space=pltpu.SMEM)
    shape = jax.ShapeDtypeStruct
    return pl.pallas_call(
        finish_kernel,
        out_shape=(shape((ROWS, D), BF16), shape((GROUP, PART, D), F32)),
        in_specs=[smem] + [vmem] * 6,
        out_specs=(vmem, vmem),
        compiler_params=pltpu.CompilerParams(vmem_limit_bytes=16 * 1024 * 1024),
    )(picks, own, from_next, from_prev, far0, far1, total)


def shards(features, w_query, w_key, w_value, w_out, cotangent, reach, picks, masks):
    count = lax.axis_size(AXIS)
    bits = count.bit_length() - 1
    up = [(i, (i + 1) % count) for i in range(count)]
    down = [(j, i) for i, j in up]
    picked = picks.reshape(1, MATCH)
    prev = lax.ppermute(features, AXIS, up)
    following = lax.ppermute(features, AXIS, down)
    halves = features.reshape(ROWS // BLOCK, BLOCK, D)
    outgoing = jnp.where(picks[:, :, None] == 0, halves[0][None], halves[1][None])
    both = jnp.sum(masks * jnp.array([1, count]))
    routes = [(both >> (m * bits)) & (count - 1) for m in range(MATCH)]
    far = crossed_both((outgoing[0], outgoing[1]), both)
    mixed, f_own, f_prev, f_next, f_far0, f_far1, partial = attend(
        picked, reach, prev, features, following, far[0], far[1], cotangent,
        w_query, w_key, w_value, w_out,
    )
    parts = exchange(partial.reshape(GROUP, PART, D))
    far0 = crossed(f_far0, routes[0], DIGIT)
    parts, far0 = lax.optimization_barrier((parts, far0))
    mine = tree([parts[i].astype(F32) for i in range(GROUP)]).astype(BF16)
    mine, f_prev, f_next = lax.optimization_barrier((mine, f_prev, f_next))
    from_next = lax.ppermute(f_prev, AXIS, down)
    from_prev = lax.ppermute(f_next, AXIS, up)
    copies = jnp.broadcast_to(summed(mine)[None], (GROUP, PART, D))
    copies, f_far1 = lax.optimization_barrier((copies, f_far1))
    total = exchange(copies)
    far1 = crossed(f_far1, routes[1], DIGIT)
    feature_grad, weight_grads = finish(picked, f_own, from_next, from_prev, far0, far1, total)
    return mixed, feature_grad, weight_grads.reshape(4, D, D)


def solution(mesh):
    return jax.shard_map(
        shards,
        mesh=mesh,
        in_specs=(
            P("blk", None),
            P(),
            P(),
            P(),
            P(),
            P("blk", None),
            P(None, "blk"),
            P(None, "blk"),
            P(),
        ),
        out_specs=(P("blk", None), P("blk", None), P()),
        check_vma=False,
    )
```

```python
import jax
import jax.numpy as jnp
from jax import lax
from jax.experimental import pallas as pl
from jax.experimental.pallas import tpu as pltpu
from jax.sharding import PartitionSpec as P

HEADS = 8
HALF = 256
BLOCK = 128
MATCH = 2
ROWS = 256
D = 384
HD = D // HEADS
NEAR = ROWS + 2 * HALF
KEYS = NEAR + MATCH * BLOCK
CHUNK = 128
FACTOR = HD ** -0.5
LOG2E = 1.4426950408889634
AXIS = "blk"
PLANE = 16
LINE = 16
GROUP = 32
PART = 4 * D // GROUP
DIGIT = 4
F32 = jnp.float32
BF16 = jnp.bfloat16


def nn(a, b):
    return lax.dot_general(a, b, (((1,), (0,)), ((), ())), preferred_element_type=F32)


def nt(a, b):
    return lax.dot_general(a, b, (((1,), (1,)), ((), ())), preferred_element_type=F32)


def tn(a, b):
    return lax.dot_general(a, b, (((0,), (0,)), ((), ())), preferred_element_type=F32)


def attend_kernel(
    picks_ref, reach_ref, prev_ref, own_ref, next_ref, far0_ref, far1_ref, cot_ref,
    wq_ref, wk_ref, wv_ref, wo_ref,
    mixed_ref, f_own_ref, f_prev_ref, f_next_ref, f_far0_ref, f_far1_ref, wg_ref,
    xt, qt, dt, kt, vt, bias, s_ref, dp_ref, pb, dsb, ot, dqt, dkt, dvt, ft,
):
    own = slice(HALF, HALF + ROWS)
    starts = (0, HALF, HALF + ROWS, NEAR, NEAR + BLOCK)
    for start, piece in zip(starts, (prev_ref, own_ref, next_ref, far0_ref, far1_ref)):
        xt[:, start:start + piece.shape[0]] = piece[...].T
    qt[...] = nn(wq_ref[...].T, xt[:, own]).astype(BF16)
    dt[...] = nt(wo_ref[...], cot_ref[...]).astype(BF16)
    kt[...] = nn(wk_ref[...].T, xt[...]).astype(BF16)
    vt[...] = nn(wv_ref[...].T, xt[...]).astype(BF16)

    rows = lax.broadcasted_iota(jnp.int32, (CHUNK, ROWS), 1)
    cols = lax.broadcasted_iota(jnp.int32, (CHUNK, ROWS), 0)
    offset = cols - HALF - rows
    back = -reach_ref[0:1, :]
    ahead = reach_ref[1:2, :]

    def near_bias(c, _):
        start = pl.multiple_of(c * CHUNK, CHUNK)
        allowed = (offset >= back - start) & (offset <= ahead - start)
        bias[pl.ds(start, CHUNK), :] = jnp.where(allowed, 0.0, -1e30)
        return 0

    lax.fori_loop(0, NEAR // CHUNK, near_bias, 0)

    halves = [slice(0, BLOCK), slice(BLOCK, ROWS)]
    near = [(c, b) for c in range(NEAR // CHUNK) for b in range(2) if b * BLOCK <= c * CHUNK <= b * BLOCK + 2 * HALF]
    picked = [picks_ref[0, m] for m in range(MATCH)]
    far_rows = [pl.ds(pl.multiple_of(picked[m] * BLOCK, BLOCK), BLOCK) for m in range(MATCH)]
    tiles = [(slice(c * CHUNK, (c + 1) * CHUNK), halves[b], b, None) for c, b in near]
    for m in range(MATCH):
        tiles.append((slice(NEAR + m * BLOCK, NEAR + (m + 1) * BLOCK), far_rows[m], None, m))
    for ref in (pb, dsb):
        ref[0:CHUNK, halves[1]] = jnp.zeros((CHUNK, BLOCK), BF16)
        ref[NEAR - CHUNK:NEAR, halves[0]] = jnp.zeros((CHUNK, BLOCK), BF16)
        ref[NEAR:KEYS, :] = jnp.zeros((MATCH * BLOCK, ROWS), BF16)

    def fold(value, how):
        return how(value.reshape(CHUNK // 8, 8, BLOCK), axis=0)

    def by_rows(near_parts, far_parts, how, none):
        joined = []
        for b in range(2):
            part = near_parts[b]
            for m in range(MATCH):
                part = how(part, jnp.where(picked[m] == b, far_parts[m], none))
            joined.append(part)
        return joined

    def of_tile(joined, b, m):
        return joined[b] if m is None else jnp.where(picked[m] == 0, joined[0], joined[1])

    def one_head(h, _):
        at = pl.ds(pl.multiple_of(h * HD, HD), HD)
        tops, far_tops = [jnp.full((8, BLOCK), -3e38, F32)] * 2, [None] * MATCH
        for c, r, b, m in tiles:
            s = tn(kt[at, c], qt[at, r])
            if m is None:
                s += bias[c, r]
                tops[b] = jnp.maximum(tops[b], fold(s, jnp.max))
            else:
                far_tops[m] = fold(s, jnp.max)
            s_ref[c, r] = s
        tops = [jnp.max(t, axis=0, keepdims=True) for t in by_rows(tops, far_tops, jnp.maximum, -3e38)]
        sums, far_sums = [jnp.zeros((8, BLOCK), F32)] * 2, [None] * MATCH
        inner, far_inner = [jnp.zeros((8, BLOCK), F32)] * 2, [None] * MATCH
        for c, r, b, m in tiles:
            e = jnp.exp2((s_ref[c, r] - of_tile(tops, b, m)) * (FACTOR * LOG2E))
            s_ref[c, r] = e
            dp = tn(vt[at, c], dt[at, r])
            dp_ref[c, r] = dp
            total, weighted = fold(e, jnp.sum), fold(e * dp, jnp.sum)
            if m is None:
                sums[b] += total
                inner[b] += weighted
            else:
                far_sums[m], far_inner[m] = total, weighted
        sums = by_rows(sums, far_sums, jnp.add, 0.0)
        inner = by_rows(inner, far_inner, jnp.add, 0.0)
        inverse = [1.0 / jnp.sum(t, axis=0, keepdims=True) for t in sums]
        mean = [jnp.sum(t, axis=0, keepdims=True) * i for t, i in zip(inner, inverse)]
        for c, r, b, m in tiles:
            p = s_ref[c, r] * of_tile(inverse, b, m)
            pb[c, r] = p.astype(BF16)
            dsb[c, r] = (p * (dp_ref[c, r] - of_tile(mean, b, m)) * FACTOR).astype(BF16)
        ot[at, :] = nn(vt[at, :], pb[...]).astype(BF16)
        dvt[at, :] = nt(dt[at, :], pb[...]).astype(BF16)
        dqt[at, :] = nn(kt[at, :], dsb[...]).astype(BF16)
        dkt[at, :] = nt(qt[at, :], dsb[...]).astype(BF16)
        return 0

    lax.fori_loop(0, HEADS, one_head, 0)

    mixed_ref[...] = tn(ot[...], wo_ref[...]).astype(BF16)
    ft[...] = nn(wk_ref[...], dkt[...]) + nn(wv_ref[...], dvt[...])
    f_own_ref[...] = (ft[:, own] + nn(wq_ref[...], dqt[...])).T
    for start, ref in zip(starts, (f_prev_ref, None, f_next_ref, f_far0_ref, f_far1_ref)):
        if ref is not None:
            ref[...] = ft[:, start:start + ref.shape[0]].astype(BF16).T
    scale = float(ROWS * 256) ** -0.5
    wg_ref[0:D, :] = (nt(xt[:, own], dqt[...]) * scale).astype(BF16)
    wg_ref[D:2 * D, :] = (nt(xt[...], dkt[...]) * scale).astype(BF16)
    wg_ref[2 * D:3 * D, :] = (nt(xt[...], dvt[...]) * scale).astype(BF16)
    wg_ref[3 * D:4 * D, :] = (nn(ot[...], cot_ref[...]) * scale).astype(BF16)


def attend(picks, reach, prev, own, following, far0, far1, cot, wq, wk, wv, wo):
    vmem = pl.BlockSpec(memory_space=pltpu.VMEM)
    smem = pl.BlockSpec(memory_space=pltpu.SMEM)
    shape = jax.ShapeDtypeStruct
    return pl.pallas_call(
        attend_kernel,
        out_shape=(
            shape((ROWS, D), BF16),
            shape((ROWS, D), F32),
            shape((HALF, D), BF16),
            shape((HALF, D), BF16),
            shape((BLOCK, D), BF16),
            shape((BLOCK, D), BF16),
            shape((4 * D, D), BF16),
        ),
        in_specs=[smem] + [vmem] * 11,
        out_specs=(vmem,) * 7,
        scratch_shapes=[
            pltpu.VMEM((D, KEYS), BF16),
            pltpu.VMEM((D, ROWS), BF16),
            pltpu.VMEM((D, ROWS), BF16),
            pltpu.VMEM((D, KEYS), BF16),
            pltpu.VMEM((D, KEYS), BF16),
            pltpu.VMEM((NEAR, ROWS), F32),
            pltpu.VMEM((KEYS, ROWS), F32),
            pltpu.VMEM((KEYS, ROWS), F32),
            pltpu.VMEM((KEYS, ROWS), BF16),
            pltpu.VMEM((KEYS, ROWS), BF16),
            pltpu.VMEM((D, ROWS), BF16),
            pltpu.VMEM((D, ROWS), BF16),
            pltpu.VMEM((D, KEYS), BF16),
            pltpu.VMEM((D, KEYS), BF16),
            pltpu.VMEM((D, KEYS), F32),
        ],
        compiler_params=pltpu.CompilerParams(vmem_limit_bytes=40 * 1024 * 1024),
        cost_estimate=pl.CostEstimate(
            flops=8_000_000_000, bytes_accessed=8_000_000, transcendentals=HEADS * KEYS * ROWS
        ),
    )(picks, reach, prev, own, following, far0, far1, cot, wq, wk, wv, wo)


def crossed(block, mask, digit):
    count = lax.axis_size(AXIS)
    bits = count.bit_length() - 1

    def move(offset):
        pairs = [(i, i ^ offset) for i in range(count)]
        return lambda piece: lax.ppermute(piece, AXIS, pairs) if offset else piece

    for low in range(0, bits, digit):
        value = (mask >> low) & ((1 << digit) - 1)
        block = lax.switch(value, [move(i << low) for i in range(1 << digit)], block)
    return block


def crossed_both(blocks, masks):
    bits = lax.axis_size(AXIS).bit_length() - 1

    def step(_, state):
        first, second, masks = state
        return second, crossed(first, masks & ((1 << bits) - 1), DIGIT), masks >> bits

    return lax.fori_loop(0, MATCH, step, (*blocks, masks))[:MATCH]


def across(block, offset):
    return lax.ppermute(block, AXIS, [(i, i ^ offset) for i in range(lax.axis_size(AXIS))])


def tree(values):
    while len(values) > 1:
        values = [a + b for a, b in zip(values[::2], values[1::2])]
    return values[0]


def exchange(parts):
    low = GROUP // PLANE
    groups = [[i * LINE + j * low + k for i in range(PLANE) for k in range(low)] for j in range(LINE // low)]
    return lax.all_to_all(parts, AXIS, 0, 0, axis_index_groups=groups)


def summed(mine):
    low = GROUP // PLANE
    for step, ways in ((low, 4), (4 * low, LINE // (4 * low))):
        terms = [mine] + [across(mine, o * step) for o in range(1, ways)]
        mine = tree([term.astype(F32) for term in terms]).astype(BF16)
    return mine


def finish_kernel(picks_ref, own_ref, from_next_ref, from_prev_ref, far0_ref, far1_ref, total_ref, f_ref, wg_ref):
    far = [ref[...].astype(F32) for ref in (far0_ref, far1_ref)]
    for b in range(ROWS // BLOCK):
        span = slice(b * BLOCK, (b + 1) * BLOCK)
        value = own_ref[span, :] + from_next_ref[span, :].astype(F32) + from_prev_ref[span, :].astype(F32)
        for m in range(MATCH):
            value += jnp.where(picks_ref[0, m] == b, far[m], 0.0)
        f_ref[span, :] = value.astype(BF16)

    def widen(i, _):
        wg_ref[i] = total_ref[i].astype(F32)
        return 0

    lax.fori_loop(0, GROUP, widen, 0)


def finish(picks, own, from_next, from_prev, far0, far1, total):
    vmem = pl.BlockSpec(memory_space=pltpu.VMEM)
    smem = pl.BlockSpec(memory_space=pltpu.SMEM)
    shape = jax.ShapeDtypeStruct
    return pl.pallas_call(
        finish_kernel,
        out_shape=(shape((ROWS, D), BF16), shape((GROUP, PART, D), F32)),
        in_specs=[smem] + [vmem] * 6,
        out_specs=(vmem, vmem),
        compiler_params=pltpu.CompilerParams(vmem_limit_bytes=16 * 1024 * 1024),
    )(picks, own, from_next, from_prev, far0, far1, total)


def shards(features, w_query, w_key, w_value, w_out, cotangent, reach, picks, masks):
    count = lax.axis_size(AXIS)
    bits = count.bit_length() - 1
    up = [(i, (i + 1) % count) for i in range(count)]
    down = [(j, i) for i, j in up]
    picked = picks.reshape(1, MATCH)
    prev = lax.ppermute(features, AXIS, up)
    following = lax.ppermute(features, AXIS, down)
    halves = features.reshape(ROWS // BLOCK, BLOCK, D)
    outgoing = jnp.where(picks[:, :, None] == 0, halves[0][None], halves[1][None])
    both = jnp.sum(masks * jnp.array([1, count]))
    routes = [(both >> (m * bits)) & (count - 1) for m in range(MATCH)]
    far = crossed_both((outgoing[0], outgoing[1]), both)
    mixed, f_own, f_prev, f_next, f_far0, f_far1, partial = attend(
        picked, reach, prev, features, following, far[0], far[1], cotangent,
        w_query, w_key, w_value, w_out,
    )
    parts = exchange(partial.reshape(GROUP, PART, D))
    far0 = crossed(f_far0, routes[0], DIGIT)
    parts, far0 = lax.optimization_barrier((parts, far0))
    mine = tree([parts[i].astype(F32) for i in range(GROUP)]).astype(BF16)
    mine, f_prev, f_next = lax.optimization_barrier((mine, f_prev, f_next))
    from_next = lax.ppermute(f_prev, AXIS, down)
    from_prev = lax.ppermute(f_next, AXIS, up)
    copies = jnp.broadcast_to(summed(mine)[None], (GROUP, PART, D))
    copies, f_far1, from_next, from_prev = lax.optimization_barrier((copies, f_far1, from_next, from_prev))
    total = exchange(copies)
    far1 = crossed(f_far1, routes[1], DIGIT)
    feature_grad, weight_grads = finish(picked, f_own, from_next, from_prev, far0, far1, total)
    return mixed, feature_grad, weight_grads.reshape(4, D, D)


def solution(mesh):
    return jax.shard_map(
        shards,
        mesh=mesh,
        in_specs=(
            P("blk", None),
            P(),
            P(),
            P(),
            P(),
            P("blk", None),
            P(None, "blk"),
            P(None, "blk"),
            P(),
        ),
        out_specs=(P("blk", None), P("blk", None), P()),
        check_vma=False,
    )
```
